256 devices in a mesh: lat: 8 (over x_hi, y), lon: 32 (over x_lo, z, core).
Axes of the slice: x: 4 (x_hi: 2, x_lo: 2; x = x_hi * 2 + x_lo), y: 4, z: 8, core: 2. Of those that a mesh axis runs over, the one named last changes fastest.
Arguments:
- tracers: float32 [2, 3, 2048, 4096], P(None, None, 'lat', 'lon'), may hold values from -6 to 6
- east_courant: float32 [3, 2048, 4096], P(None, 'lat', 'lon'), may hold values from -0.45 to 0.45
- north_courant: float32 [3, 2048, 4096], P(None, 'lat', 'lon'), may hold values from -0.45 to 0.45
- east_kappa: float32 [3, 2048, 4096], P(None, 'lat', 'lon'), may hold values from 0.01 to 0.1
- north_kappa: float32 [3, 2048, 4096], P(None, 'lat', 'lon'), may hold values from 0.01 to 0.1
- ocean_mask: int32 [3, 2048, 4096], P(None, 'lat', 'lon'), may hold values 0 or 1
- fold_map: int32 [4096], P('lon'), may hold values from 0 to 4095, as said below
Outputs:
- updated: float32 [2, 3, 2048, 4096], P(None, None, 'lat', 'lon')
The draws below stay inside these ranges and needn't reach their ends.
Inputs may be any that keep to these rules, and one draw needn't show every extreme that they name: fold_map[i] = (P - 1 - i) mod 4096 for every column i, with one pivot P that is a multiple of 128.
All inputs are finite; a program needn't handle non-finite values. No bound on the sum of `ocean_mask` on one device may be relied on, other than what follows from the above.
Results may differ from the reference program's by a relative error of at most 0.00002.
Values sent between devices are 32-bit elements; how exact they have to be, the bound alone decides.
No kernel may reach another device: no remote copies, remote signals or barrier semaphores. Data moves between devices by JAX's collectives and lax.ppermute only.
A program may use at most 64 MiB of HBM per device.

```python
import math
import jax
import jax.numpy as jnp
from jax import lax

LEV = 3
STEPS = 2
CLON = 128
NY = 2048
NX = 4096


def draw_fold_map(key, part):
    blocks = NX // CLON
    pivot = jax.random.randint(key, (), 0, blocks, dtype=jnp.int32) * CLON
    column = jnp.arange(NX, dtype=jnp.int32)
    return ((pivot - 1 - column) % NX).astype(jnp.int32)


def plant(values, rng, low, largest):
    dims = values.shape
    place = [jax.random.randint(jax.random.fold_in(rng, axis), (), 0, dims[axis]) for axis in range(len(dims))]
    values = values.at[tuple(place)].set(low)
    longest = dims.index(max(dims))
    place[longest] = (place[longest] + 1) % dims[longest]
    return values.at[tuple(place)].set(largest)


def steps_of(rng, extent, shards, smallest, largest):
    def one(position, parts):
        heights = jax.random.uniform(jax.random.fold_in(jax.random.fold_in(rng, 6), position), (parts,), jnp.float32, smallest / len(shards), largest / len(shards))
        return jnp.repeat(jnp.exp(heights), extent[position] // parts).reshape((-1,) + (1,) * (len(extent) - position - 1))

    gain = one(*shards[0])
    for cut in shards[1:]:
        gain = gain * one(*cut)
    return gain


def normal_values(stream_key, dims, deviation, reach, cuts=(), kind=jnp.bfloat16):
    level = steps_of(stream_key, dims, cuts, -0.22, 0.18) if cuts else 1.0
    drawn = jax.random.normal(stream_key, dims, jnp.float32) * deviation * level
    return jnp.minimum(jnp.maximum(drawn, -reach), reach).astype(kind)


def setup_inputs(seed: int = 0) -> dict:
    keys = jax.random.split(jax.random.key(seed), 8)
    tracers = normal_values(keys[0], (2, LEV, NY, NX), 1.0, 6.0, ((2, 8), (3, 32)), jnp.float32)
    east_courant = jnp.clip(jax.random.uniform(keys[1], (LEV, NY, NX), jnp.float32, -0.45, 0.45) * steps_of(keys[1], (LEV, NY, NX), ((1, 8), (2, 32)), -0.4, 0.0), -0.45, 0.45)
    north_courant = jnp.clip(jax.random.uniform(keys[2], (LEV, NY, NX), jnp.float32, -0.45, 0.45) * steps_of(keys[2], (LEV, NY, NX), ((1, 8), (2, 32)), -0.4, 0.0), -0.45, 0.45)
    east_kappa = jnp.clip(jnp.exp(math.log(0.1) - 2.3025851 * jax.random.uniform(keys[3], (LEV, NY, NX), jnp.float32) ** steps_of(keys[3], (LEV, NY, NX), ((1, 8), (2, 32)), -0.2, 0.2)), 0.01, 0.1)
    north_kappa = jnp.clip(jnp.exp(math.log(0.1) - 2.3025851 * jax.random.uniform(keys[4], (LEV, NY, NX), jnp.float32) ** steps_of(keys[4], (LEV, NY, NX), ((1, 8), (2, 32)), -0.2, 0.2)), 0.01, 0.1)
    ocean_mask = plant((jax.random.randint(keys[5], (LEV, NY, NX), 0, 5) < 4).astype(jnp.int32), jax.random.fold_in(keys[5], 1), 0, 1)
    fold_map = draw_fold_map(jax.random.fold_in(keys[7], 71), 0)
    return {"tracers": tracers, "east_courant": east_courant, "north_courant": north_courant, "east_kappa": east_kappa, "north_kappa": north_kappa, "ocean_mask": ocean_mask, "fold_map": fold_map}


def face_flux(behind, center, forward, beyond, courant, diffusivity, opened):
    centered = 7.0 * (center + forward) - (behind + beyond)
    upwind = 3.0 * (forward - center) - (beyond - behind)
    return opened * (courant * centered / 12.0 - jnp.abs(courant) * upwind / 12.0 - diffusivity * (forward - center))


def advance(state, ocean, east_c, east_k, open_east, north_c, north_k, open_north, fold_map):
    width = state.shape[2]
    along = jnp.concatenate([state[:, :, -2:], state, state[:, :, :2]], axis=2)
    folded = jnp.stack([state[:, -1, :][:, fold_map], state[:, -2, :][:, fold_map]], axis=1)
    across = jnp.concatenate([jnp.zeros((2, 2, width), jnp.float32), state, folded], axis=1)
    east_flux = face_flux(along[:, :, :-3], along[:, :, 1:-2], along[:, :, 2:-1], along[:, :, 3:], east_c, east_k, open_east)
    north_flux = face_flux(across[:, :-3], across[:, 1:-2], across[:, 2:-1], across[:, 3:], north_c, north_k, open_north)
    return ocean * (state - (east_flux[:, :, 1:] - east_flux[:, :, :-1]) - (north_flux[:, 1:] - north_flux[:, :-1]))


def reference(tracers, east_courant, north_courant, east_kappa, north_kappa, ocean_mask, fold_map):
    def one_level(level_index):
        def pick(field):
            return lax.dynamic_index_in_dim(field, level_index, 0, keepdims=False)

        state = lax.dynamic_index_in_dim(tracers, level_index, 1, keepdims=False)
        ocean = pick(ocean_mask).astype(jnp.float32)
        width = ocean.shape[1]
        zero_row = jnp.zeros((1, width), jnp.float32)
        east_cour = pick(east_courant)
        east_diff = pick(east_kappa)
        east_c = jnp.concatenate([east_cour[:, -1:], east_cour], axis=1)
        east_k = jnp.concatenate([east_diff[:, -1:], east_diff], axis=1)
        beside = jnp.concatenate([ocean[:, -1:], ocean, ocean[:, :1]], axis=1)
        open_east = beside[:, :-1] * beside[:, 1:]
        north_c = jnp.concatenate([zero_row, pick(north_courant)], axis=0)
        north_k = jnp.concatenate([zero_row, pick(north_kappa)], axis=0)
        vertical = jnp.concatenate([zero_row, ocean, ocean[-1:]], axis=0)
        open_north = vertical[:-1] * vertical[1:]
        state = state * ocean
        for step_index in range(STEPS):
            state = advance(state, ocean, east_c, east_k, open_east, north_c, north_k, open_north, fold_map)
        return state

    result = lax.map(one_level, jnp.arange(LEV, dtype=jnp.int32))
    return jnp.transpose(result, (1, 0, 2, 3))
```

```python
import functools

import jax
import jax.numpy as jnp
from jax import lax
from jax.experimental import pallas as pl
from jax.experimental.pallas import tpu as pltpu
from jax.sharding import PartitionSpec as P

BOTH = ("lat", "lon")
LEV = 3
MEM = 6
ROWS = 256
BLOCKS = 8
GROUPS = 4
F32 = jnp.float32


def lanes():
    return lax.broadcasted_iota(jnp.int32, (8, 128), 1)


def roll(x, shift):
    shift = shift % 128
    return x if shift == 0 else pltpu.roll(x, shift, axis=1)


def face(courant, kappa):
    size = jnp.abs(courant)
    slope = 3.0 * size + kappa
    seven = 7.0 * courant
    return -(courant + size), seven + slope, seven - slope, size - courant


def weigh(ocean, east, west, north, south):
    ea, eb, ec, ed = face(*east)
    wa, wb, wc, wd = face(*west)
    na, nb, nc, nd = face(*north)
    sa, sb, sc, sd = face(*south)
    return (
        ocean * (1.0 + (wc - eb) + (sc - nb)),
        ocean * wa,
        ocean * (wb - ea),
        ocean * (wd - ec),
        -(ocean * ed),
        ocean * sa,
        ocean * (sb - na),
        ocean * (sd - nc),
        -(ocean * nd),
    )


def apply(w, q, sides, below2, below1, above1, above2, lane):
    west2 = roll(jnp.where(lane >= 126, sides, q), 2)
    west1 = roll(jnp.where(lane == 127, sides, q), 1)
    east1 = roll(jnp.where(lane == 0, sides, q), -1)
    east2 = roll(jnp.where(lane < 2, sides, q), -2)
    across = (w[1] * west2 + w[2] * west1) + (w[3] * east1 + w[4] * east2)
    along = (w[5] * below2 + w[6] * below1) + (w[7] * above1 + w[8] * above2)
    return w[0] * q + (across + along)


def place(kept, x, source, target, count, lane):
    moved = roll(x, target - source)
    if count == 1:
        here = lane == target
    else:
        here = (lane >= target) & (lane < target + count)
    return jnp.where(here, moved, kept)


def rows_of(i, g):
    return pl.ds(pl.multiple_of(i * 8, 8) + 64 * g, 8)


def pack_kernel(t_ref, ue_ref, un_ref, ke_ref, kn_ref, m_ref, a_ref, b_ref, e_ref, w_ref, nb, sb):
    lane = lanes()
    nb[...] = jnp.zeros((64, 128), F32)
    sb[...] = jnp.zeros((64, 128), F32)
    for lev in range(LEV):
        base = 24 + 12 * lev
        for out, lo, rows, faces in ((nb, ROWS - 8, slice(6, 8), slice(5, 7)), (sb, 0, slice(0, 2), slice(0, 2))):
            tile = pl.ds(lo, 8)
            ocean = m_ref[lev, tile].astype(F32)
            beside = jnp.where(lane == 127, 1.0, roll(ocean, -1))
            up = slice(faces.start + 1, faces.stop + 1)
            shut = ocean[faces] * ocean[up]
            un = un_ref[lev, tile] * (1.0 / 12.0)
            kn = kn_ref[lev, tile]
            out[base : base + 2] = un[faces] * shut
            out[base + 3 : base + 5] = kn[faces] * shut
            if lo:
                out[base + 2 : base + 3] = un[7:8] * ocean[7:8]
                out[base + 5 : base + 6] = kn[7:8] * ocean[7:8]
            open_e = ocean * beside
            out[base + 6 : base + 8] = (ue_ref[lev, tile] * (1.0 / 12.0) * open_e)[rows]
            out[base + 8 : base + 10] = (ke_ref[lev, tile] * open_e)[rows]
            out[base + 10 : base + 12] = ocean[rows]
            for t in range(2):
                q = t_ref[t, lev, tile] * ocean
                m = 3 * t + lev
                out[4 * m : 4 * m + 4] = q[4:8] if lo else q[0:4]
    even = lax.rem(lax.axis_index("lat"), 2) == 0
    north, south = nb[...], sb[...]
    a_ref[...] = jnp.where(even, north, south)
    b_ref[...] = jnp.where(even, south, north)

    def body(i, carry):
        to_e = jnp.zeros((8, 128), F32)
        to_w = jnp.zeros((8, 128), F32)
        for g in range(GROUPS):
            blk = rows_of(i, g)
            for lev in range(LEV):
                ocean = m_ref[lev, blk].astype(F32)
                u = ue_ref[lev, blk] * (1.0 / 12.0) * ocean
                k = ke_ref[lev, blk] * ocean
                at = 32 * g + 24 + lev
                to_e = place(to_e, u, 127, at, 1, lane)
                to_e = place(to_e, k, 127, at + 3, 1, lane)
                to_w = place(to_w, ocean, 0, at, 1, lane)
                for t in range(2):
                    q = t_ref[t, lev, blk] * ocean
                    at = 32 * g + 4 * (3 * t + lev)
                    to_e = place(to_e, q, 126, at, 2, lane)
                    to_w = place(to_w, q, 0, at + 2, 2, lane)
        out = pl.ds(pl.multiple_of(i * 8, 8), 8)
        e_ref[out] = to_e
        w_ref[out] = to_w
        return carry

    lax.fori_loop(0, BLOCKS, body, 0)


def flip(x):
    lane = lax.broadcasted_iota(jnp.int32, x.shape, 1)
    for s in (1, 2, 4, 8, 16, 32, 64):
        x = jnp.where((lane & s) != 0, roll(x, s), roll(x, -s))
    return x


def step_kernel(
    t_ref, ue_ref, un_ref, ke_ref, kn_ref, m_ref, re_ref, rw_ref, ra_ref, rb_ref,
    wt_ref, q1_ref, hc_ref, hq_ref, e_ref, w_ref,
    q0, os, nu, nk, nh, sh,
):
    lane = lanes()
    lat = lax.axis_index("lat")
    even = lax.rem(lat, 2) == 0
    southern = lat == 0
    northern = lat == lax.axis_size("lat") - 1
    first, second = ra_ref[...], rb_ref[...]
    sh[...] = jnp.where(southern, 0.0, jnp.where(even, second, first))
    nh[...] = jnp.where(even, first, second)

    @pl.when(northern)
    def _():
        f = flip(rb_ref[...])
        shifted = roll(f, -1)
        for m in range(MEM):
            for r in range(4):
                nh[4 * m + r : 4 * m + r + 1] = f[4 * m + 3 - r : 4 * m + 4 - r]
        for lev in range(LEV):
            base = 24 + 12 * lev
            for to, source, x in (
                (0, 1, -f), (1, 0, -f), (2, 2, -f), (3, 4, f), (4, 3, f), (5, 5, f),
                (6, 7, -shifted), (7, 6, -shifted), (8, 9, shifted), (9, 8, shifted), (10, 11, f), (11, 10, f),
            ):
                nh[base + to : base + to + 1] = x[base + source : base + source + 1]

    for m in range(MEM):
        q0[m, 4:8] = sh[4 * m : 4 * m + 4]
        q0[m, 264:268] = nh[4 * m : 4 * m + 4]

    def fill(i, carry):
        blk = pl.ds(pl.multiple_of(i * 8, 8), 8)
        own = pl.ds(pl.multiple_of(i * 8, 8) + 8, 8)
        for lev in range(LEV):
            ocean = m_ref[lev, blk].astype(F32)
            os[lev, own] = ocean
            for t in range(2):
                q0[3 * t + lev, own] = t_ref[t, lev, blk] * ocean
        return carry

    lax.fori_loop(0, ROWS // 8, fill, 0)
    for lev in range(LEV):
        base = 24 + 12 * lev
        top = os[lev, 263:264]
        os[lev, 264:265] = jnp.where(northern, top, nh[base + 10 : base + 11])
        low = os[lev, 8:9]
        nu[lev, 7:8] = sh[base + 2 : base + 3] * low
        nk[lev, 7:8] = sh[base + 5 : base + 6] * low

    def faces(i, carry):
        at = pl.multiple_of(i * 8, 8)
        blk, own, above = pl.ds(at, 8), pl.ds(at + 8, 8), pl.ds(at + 9, 8)
        for lev in range(LEV):
            shut = os[lev, own] * os[lev, above]
            nu[lev, own] = un_ref[lev, blk] * (1.0 / 12.0) * shut
            nk[lev, own] = kn_ref[lev, blk] * shut
        return carry

    lax.fori_loop(0, ROWS // 8, faces, 0)

    def body(i, carry):
        at = pl.multiple_of(i * 8, 8)
        out = pl.ds(at, 8)
        from_w, from_e = re_ref[out], rw_ref[out]
        both = jnp.where((lane & 2) == 0, from_w, from_e)
        to_e = jnp.zeros((8, 128), F32)
        to_w = jnp.zeros((8, 128), F32)
        for g in range(GROUPS):
            blk = rows_of(i, g)

            def near(k, at=at, g=g):
                return pl.ds(at + (64 * g + 8 + k), 8)

            for lev in range(LEV):
                ocean = os[lev, near(0)]
                spot = 32 * g + 24 + lev
                beside = jnp.where(lane == 127, roll(from_e, 127 - spot), roll(ocean, -1))
                shut = ocean * beside
                u = ue_ref[lev, blk] * (1.0 / 12.0) * shut
                k = ke_ref[lev, blk] * shut
                uw = jnp.where(lane == 0, roll(from_w, -spot) * ocean, roll(u, 1))
                kw = jnp.where(lane == 0, roll(from_w, -(spot + 3)) * ocean, roll(k, 1))
                north = nu[lev, near(0)], nk[lev, near(0)]
                south = nu[lev, near(-1)], nk[lev, near(-1)]
                w = weigh(ocean, (u, k), (uw, kw), north, south)
                for n in range(9):
                    wt_ref[9 * lev + n, blk] = w[n]
                for t in range(2):
                    m = 3 * t + lev
                    spot = 32 * g + 4 * m
                    sides = roll(both, 126 - spot)
                    new = apply(
                        w, q0[m, near(0)], sides, q0[m, near(-2)], q0[m, near(-1)], q0[m, near(1)], q0[m, near(2)], lane
                    )
                    q1_ref[m, blk] = new
                    to_e = place(to_e, new, 126, spot, 2, lane)
                    to_w = place(to_w, new, 0, spot + 2, 2, lane)
        e_ref[out] = to_e
        w_ref[out] = to_w
        return carry

    lax.fori_loop(0, BLOCKS, body, 0)

    hc_ref[...] = jnp.zeros((7 * LEV, 8, 128), F32)
    hq_ref[...] = jnp.zeros((5 * MEM, 8, 128), F32)
    for lev in range(LEV):
        base = 24 + 12 * lev
        for n, (ref, slot) in enumerate(((nu, 0), (nk, 3))):
            lower = jnp.where(northern, nh[base + slot + 2 : base + slot + 3], ref[lev, 263:264])
            hc_ref[7 * lev + n, 0:2] = sh[base + slot : base + slot + 2]
            hc_ref[7 * lev + n, 2:3] = lower
            hc_ref[7 * lev + n, 3:4] = nh[base + slot : base + slot + 1]
            hc_ref[7 * lev + 2 + n, 0:1] = sh[base + slot + 1 : base + slot + 2]
            hc_ref[7 * lev + 2 + n, 1:2] = ref[lev, 7:8]
            hc_ref[7 * lev + 2 + n, 2:4] = nh[base + slot : base + slot + 2]
        for n in range(3):
            hc_ref[7 * lev + 4 + n, 0:2] = sh[base + 6 + 2 * n : base + 8 + 2 * n]
            hc_ref[7 * lev + 4 + n, 2:4] = nh[base + 6 + 2 * n : base + 8 + 2 * n]
    for m in range(MEM):
        for k in range(5):
            hq_ref[6 * k + m, 0:2] = q0[m, 4 + k : 6 + k]
            hq_ref[6 * k + m, 2:4] = q0[m, 262 + k : 264 + k]
    to_e = jnp.zeros((8, 128), F32)
    to_w = jnp.zeros((8, 128), F32)
    for m in range(MEM):
        q = hq_ref[12 + m]
        to_e = place(to_e, q, 126, 4 * m, 2, lane)
        to_w = place(to_w, q, 0, 4 * m + 2, 2, lane)
    for lev in range(LEV):
        u, k, ocean = hc_ref[7 * lev + 4], hc_ref[7 * lev + 5], hc_ref[7 * lev + 6]
        for x, spot in ((u, 32), (k, 35), (ocean, 38)):
            to_e = place(to_e, x, 127, spot + lev, 1, lane)
            to_w = place(to_w, x, 0 if spot == 38 else 127, spot + lev, 1, lane)
    e_ref[64:72] = to_e
    w_ref[64:72] = to_w


def last_kernel(wt_ref, q1_ref, hc_ref, hq_ref, re_ref, rw_ref, out_ref, qs):
    lane = lanes()
    row = lax.broadcasted_iota(jnp.int32, (8, 128), 0)
    northern = lax.axis_index("lat") == lax.axis_size("lat") - 1
    folded = (row >= 2) & northern

    def fill(i, carry):
        blk = pl.ds(pl.multiple_of(i * 8, 8), 8)
        own = pl.ds(pl.multiple_of(i * 8, 8) + 8, 8)
        for m in range(MEM):
            qs[m, own] = q1_ref[m, blk]
        return carry

    lax.fori_loop(0, ROWS // 8, fill, 0)
    from_w, from_e = re_ref[64:72], rw_ref[64:72]
    both = jnp.where((lane & 2) == 0, from_w, from_e)
    for lev in range(LEV):
        ulo, klo, uup, kup, u, k, ocean = (hc_ref[7 * lev + n] for n in range(7))
        ocean_w = roll(from_w, -(38 + lev))
        ocean_e = roll(from_e, 127 - 38 - lev)

        def ends(x, spot, ocean=ocean, ocean_w=ocean_w, ocean_e=ocean_e):
            east = jnp.where(folded, roll(from_e, 127 - spot) * ocean, x * ocean_e)
            west = jnp.where(folded, roll(x, 1) * ocean_w, roll(from_w, -spot) * ocean)
            return jnp.where(lane == 127, east, x), jnp.where(lane == 0, west, roll(x, 1))

        ue, uw = ends(u, 32 + lev)
        ke, kw = ends(k, 35 + lev)
        w = weigh(ocean, (ue, ke), (uw, kw), (uup, kup), (ulo, klo))
        for t in range(2):
            m = 3 * t + lev
            q = [hq_ref[6 * n + m] for n in range(5)]
            new = apply(w, q[2], roll(both, 126 - 4 * m), q[0], q[1], q[3], q[4], lane)
            qs[m, 6:8] = new[0:2]
            qs[m, 264:266] = new[2:4]

    def body(i, carry):
        at = pl.multiple_of(i * 8, 8)
        both = jnp.where((lane & 2) == 0, re_ref[pl.ds(at, 8)], rw_ref[pl.ds(at, 8)])
        for g in range(GROUPS):
            blk = rows_of(i, g)

            def near(k, at=at, g=g):
                return pl.ds(at + (64 * g + 8 + k), 8)

            for lev in range(LEV):
                w = [wt_ref[9 * lev + n, blk] for n in range(9)]
                for t in range(2):
                    m = 3 * t + lev
                    sides = roll(both, 126 - 32 * g - 4 * m)
                    out_ref[t, lev, blk] = apply(
                        w, qs[m, near(0)], sides, qs[m, near(-2)], qs[m, near(-1)], qs[m, near(1)], qs[m, near(2)], lane
                    )
        return carry

    lax.fori_loop(0, BLOCKS, body, 0)


def call(kernel, shapes, scratch, name, *operands):
    vmem = pl.BlockSpec(memory_space=pltpu.VMEM)
    return pl.pallas_call(
        kernel,
        out_shape=[jax.ShapeDtypeStruct(s, F32) for s in shapes],
        in_specs=[vmem] * len(operands),
        out_specs=[vmem] * len(shapes),
        scratch_shapes=[pltpu.VMEM(s, F32) for s in scratch],
        compiler_params=pltpu.CompilerParams(vmem_limit_bytes=16 * 2**20),
        name=name,
    )(*operands)


def patterns(height, width):
    def flat(make):
        return [
            (lat * width + lon, (to[0] % height) * width + to[1] % width)
            for lat in range(height)
            for lon in range(width)
            for to in [make(lat, lon)]
        ]

    def odd(pivot):
        def make(lat, lon):
            if lat == height - 1:
                return lat, pivot - 1 - lon
            if lat == 0:
                return lat, lon
            return (lat + 1, lon) if lat % 2 else (lat - 1, lon)

        return flat(make)

    east = flat(lambda lat, lon: (lat, lon + 1))
    west = flat(lambda lat, lon: (lat, lon - 1))
    pairs = flat(lambda lat, lon: (lat + 1, lon) if lat % 2 == 0 else (lat - 1, lon))
    return east, west, pairs, odd


def local(height, width, tracers, east_courant, north_courant, east_kappa, north_kappa, ocean_mask, fold_map):
    east, west, pairs, odd = patterns(height, width)
    fields = (tracers, east_courant, north_courant, east_kappa, north_kappa, ocean_mask)
    pivot = ((fold_map[0] + 1) // 128 + lax.axis_index("lon")) % width
    edge = (64, 128)
    a, b, e, w = call(pack_kernel, [edge] * 4, [edge] * 2, "pack", *fields)
    re = lax.ppermute(e, BOTH, east)
    rw = lax.ppermute(w, BOTH, west)
    ra = lax.ppermute(a, BOTH, pairs)
    rb = lax.switch(pivot, [lambda x, p=p: lax.ppermute(x, BOTH, odd(p)) for p in range(width)], b)
    ext = (LEV, ROWS + 16, 128)
    wt, q1, hc, hq, e, w = call(
        step_kernel,
        [(9 * LEV, ROWS, 128), (MEM, ROWS, 128), (7 * LEV, 8, 128), (5 * MEM, 8, 128), (72, 128), (72, 128)],
        [(MEM, ROWS + 16, 128), ext, ext, ext, edge, edge],
        "step",
        *fields, re, rw, ra, rb,
    )
    re = lax.ppermute(e, BOTH, east)
    rw = lax.ppermute(w, BOTH, west)
    [out] = call(last_kernel, [(2, LEV, ROWS, 128)], [(MEM, ROWS + 16, 128)], "last", wt, q1, hc, hq, re, rw)
    return out


def solution(mesh):
    plane = P(None, "lat", "lon")
    grid = P(None, None, "lat", "lon")
    return jax.shard_map(
        functools.partial(local, mesh.shape["lat"], mesh.shape["lon"]),
        mesh=mesh,
        in_specs=(grid, plane, plane, plane, plane, plane, P("lon")),
        out_specs=grid,
        check_vma=False,
    )
```

```python
import functools

import jax
import jax.numpy as jnp
from jax import lax
from jax.experimental import pallas as pl
from jax.experimental.pallas import tpu as pltpu
from jax.sharding import PartitionSpec as P

BOTH = ("lat", "lon")
LEV = 3
MEM = 6
ROWS = 256
BLOCKS = 8
GROUPS = 4
TWELFTH = 1.0 / 12.0
F32 = jnp.float32


def lanes():
    return lax.broadcasted_iota(jnp.int32, (8, 128), 1)


def roll(x, shift):
    shift = shift % 128
    return x if shift == 0 else pltpu.roll(x, shift, axis=1)


def face(courant, kappa):
    size = jnp.abs(courant)
    slope = 3.0 * size + kappa
    seven = 7.0 * courant
    return -(courant + size), seven + slope, seven - slope, size - courant


def weigh(ocean, east, west, north, south):
    ea, eb, ec, ed = face(*east)
    wa, wb, wc, wd = face(*west)
    na, nb, nc, nd = face(*north)
    sa, sb, sc, sd = face(*south)
    return (
        ocean + ((wc - eb) + (sc - nb)),
        wa,
        wb - ea,
        wd - ec,
        -ed,
        sa,
        sb - na,
        sd - nc,
        -nd,
    )


def apply(w, q, sides, below2, below1, above1, above2, lane):
    west2 = roll(jnp.where(lane >= 126, sides, q), 2)
    west1 = roll(jnp.where(lane == 127, sides, q), 1)
    east1 = roll(jnp.where(lane == 0, sides, q), -1)
    east2 = roll(jnp.where(lane < 2, sides, q), -2)
    across = (w[1] * west2 + w[2] * west1) + (w[3] * east1 + w[4] * east2)
    along = (w[5] * below2 + w[6] * below1) + (w[7] * above1 + w[8] * above2)
    return w[0] * q + (across + along)


def place(kept, x, source, target, count, lane):
    moved = roll(x, target - source)
    if count == 1:
        here = lane == target
    else:
        here = (lane >= target) & (lane < target + count)
    return jnp.where(here, moved, kept)


def chunk(i, k=0):
    if isinstance(i, int):
        return pl.ds(32 * i + k, 8)
    return pl.ds(pl.multiple_of(32 * i, 32) + k, 8)


def tile(i):
    return pl.ds(8 * i, 8) if isinstance(i, int) else pl.ds(pl.multiple_of(8 * i, 8), 8)


def pack_kernel(
    t_in, ue_in, un_in, ke_in, kn_in, m_in,
    a_ref, b_ref, e_ref, w_ref, q0, os, un, kn, ue, ke,
    tv, mv, nb, sb, sems,
):
    own = pl.ds(8, ROWS)
    copies = [
        pltpu.make_async_copy(m_in, mv, sems.at[0]),
        pltpu.make_async_copy(t_in, tv, sems.at[1]),
        pltpu.make_async_copy(ue_in, ue, sems.at[2]),
        pltpu.make_async_copy(ke_in, ke, sems.at[3]),
        pltpu.make_async_copy(un_in, un.at[:, own], sems.at[4]),
        pltpu.make_async_copy(kn_in, kn.at[:, own], sems.at[5]),
    ]
    for c in copies:
        c.start()
    lane = lanes()
    nb[...] = jnp.zeros((64, 128), F32)
    sb[...] = jnp.zeros((64, 128), F32)
    for c in copies[:4]:
        c.wait()

    def body(i, carry):
        to_e = jnp.zeros((8, 128), F32)
        to_w = jnp.zeros((8, 128), F32)
        for g in range(GROUPS):
            blk, ext = chunk(i, 8 * g), chunk(i, 8 * g + 8)
            for lev in range(LEV):
                ocean = mv[lev, blk].astype(F32)
                os[lev, ext] = ocean
                at = 32 * g + 24 + lev
                to_e = place(to_e, ue[lev, blk] * ocean, 127, at, 1, lane)
                to_e = place(to_e, ke[lev, blk] * ocean, 127, at + 3, 1, lane)
                to_w = place(to_w, ocean, 0, at, 1, lane)
                for t in range(2):
                    m = 3 * t + lev
                    q = tv[t, lev, blk] * ocean
                    q0[m, ext] = q
                    at = 32 * g + 4 * m
                    to_e = place(to_e, q, 126, at, 2, lane)
                    to_w = place(to_w, q, 0, at + 2, 2, lane)
        e_ref[tile(i)] = to_e
        w_ref[tile(i)] = to_w
        return carry

    lax.fori_loop(0, BLOCKS, body, 0)
    for c in copies[4:]:
        c.wait()
    for lev in range(LEV):
        base = 24 + 12 * lev
        for out, lo, rows, faces in ((nb, ROWS - 8, slice(6, 8), slice(5, 7)), (sb, 0, slice(0, 2), slice(0, 2))):
            blk, ext = pl.ds(lo, 8), pl.ds(lo + 8, 8)
            ocean = os[lev, ext]
            beside = jnp.where(lane == 127, 1.0, roll(ocean, -1))
            up = slice(faces.start + 1, faces.stop + 1)
            shut = ocean[faces] * ocean[up]
            u, k = un[lev, ext], kn[lev, ext]
            out[base : base + 2] = u[faces] * shut
            out[base + 3 : base + 5] = k[faces] * shut
            if lo:
                out[base + 2 : base + 3] = u[7:8] * ocean[7:8]
                out[base + 5 : base + 6] = k[7:8] * ocean[7:8]
            open_e = ocean * beside
            out[base + 6 : base + 8] = (ue[lev, blk] * open_e)[rows]
            out[base + 8 : base + 10] = (ke[lev, blk] * open_e)[rows]
            out[base + 10 : base + 12] = ocean[rows]
            for t in range(2):
                m = 3 * t + lev
                q = q0[m, ext]
                out[4 * m : 4 * m + 4] = q[4:8] if lo else q[0:4]
    even = lax.rem(lax.axis_index("lat"), 2) == 0
    north, south = nb[...], sb[...]
    a_ref[...] = jnp.where(even, north, south)
    b_ref[...] = jnp.where(even, south, north)


def flip(x):
    lane = lax.broadcasted_iota(jnp.int32, x.shape, 1)
    for s in (1, 2, 4, 8, 16, 32, 64):
        x = jnp.where((lane & s) != 0, roll(x, s), roll(x, -s))
    return x


def advance(i, groups, to_e, to_w, lane, q0, os, un, kn, ue, ke, re_ref, rw_ref, wt, q1):
    from_w, from_e = re_ref[tile(i)], rw_ref[tile(i)]
    both = jnp.where((lane & 2) == 0, from_w, from_e)
    for g in groups:
        blk = chunk(i, 8 * g)

        def near(k, g=g):
            return chunk(i, 8 * g + 8 + k)

        for lev in range(LEV):
            ocean = os[lev, near(0)]
            spot = 32 * g + 24 + lev
            beside = jnp.where(lane == 127, roll(from_e, 127 - spot), roll(ocean, -1))
            shut = ocean * beside
            u = ue[lev, blk] * (shut * TWELFTH)
            k = ke[lev, blk] * shut
            uw = jnp.where(lane == 0, roll(from_w, -spot) * (ocean * TWELFTH), roll(u, 1))
            kw = jnp.where(lane == 0, roll(from_w, -(spot + 3)) * ocean, roll(k, 1))
            shut = ocean * os[lev, near(1)]
            north = un[lev, near(0)] * (shut * TWELFTH), kn[lev, near(0)] * shut
            shut = ocean * os[lev, near(-1)]
            south = un[lev, near(-1)] * (shut * TWELFTH), kn[lev, near(-1)] * shut
            w = weigh(ocean, (u, k), (uw, kw), north, south)
            for n in range(9):
                wt[9 * lev + n, blk] = w[n]
            for t in range(2):
                m = 3 * t + lev
                spot = 32 * g + 4 * m
                sides = roll(both, 126 - spot)
                new = apply(
                    w, q0[m, near(0)], sides, q0[m, near(-2)], q0[m, near(-1)], q0[m, near(1)], q0[m, near(2)], lane
                )
                q1[m, near(0)] = new
                to_e = place(to_e, new, 126, spot, 2, lane)
                to_w = place(to_w, new, 0, spot + 2, 2, lane)
    return to_e, to_w


def inner_kernel(q0, os, un, kn, ue, ke, re_ref, rw_ref, wt, q1, e_ref, w_ref):
    lane = lanes()

    def body(i, carry):
        none = jnp.zeros((8, 128), F32)
        to_e, to_w = advance(i, range(GROUPS), none, none, lane, q0, os, un, kn, ue, ke, re_ref, rw_ref, wt, q1)
        e_ref[tile(i)] = to_e
        w_ref[tile(i)] = to_w
        return carry

    lax.fori_loop(0, BLOCKS, body, 0)


def edge_kernel(
    ue, ke, re_ref, rw_ref, ra_ref, rb_ref, q0_, os_, un_, kn_, wt_, q1_, e_, w_,
    q0, os, un, kn, wt, q1, e_ref, w_ref, hc_ref, hq_ref,
    nh, sh,
):
    lane = lanes()
    lat = lax.axis_index("lat")
    even = lax.rem(lat, 2) == 0
    southern = lat == 0
    northern = lat == lax.axis_size("lat") - 1
    first, second = ra_ref[...], rb_ref[...]
    sh[...] = jnp.where(southern, 0.0, jnp.where(even, second, first))
    nh[...] = jnp.where(even, first, second)

    @pl.when(northern)
    def _():
        f = flip(rb_ref[...])
        shifted = roll(f, -1)
        for m in range(MEM):
            for r in range(4):
                nh[4 * m + r : 4 * m + r + 1] = f[4 * m + 3 - r : 4 * m + 4 - r]
        for lev in range(LEV):
            base = 24 + 12 * lev
            for to, source, x in (
                (0, 1, -f), (1, 0, -f), (2, 2, -f), (3, 4, f), (4, 3, f), (5, 5, f),
                (6, 7, -shifted), (7, 6, -shifted), (8, 9, shifted), (9, 8, shifted), (10, 11, f), (11, 10, f),
            ):
                nh[base + to : base + to + 1] = x[base + source : base + source + 1]

    for m in range(MEM):
        q0[m, 4:8] = sh[4 * m : 4 * m + 4]
        q0[m, 264:268] = nh[4 * m : 4 * m + 4]
    for lev in range(LEV):
        base = 24 + 12 * lev
        top = os[lev, 263:264]
        os[lev, 264:265] = jnp.where(northern, top, nh[base + 10 : base + 11])
        os[lev, 7:8] = sh[base + 11 : base + 12]
        un[lev, 7:8] = sh[base + 2 : base + 3]
        kn[lev, 7:8] = sh[base + 5 : base + 6]
    for i, g in ((0, 0), (BLOCKS - 1, GROUPS - 1)):
        to_e, to_w = advance(
            i, (g,), e_ref[tile(i)], w_ref[tile(i)], lane, q0, os, un, kn, ue, ke, re_ref, rw_ref, wt, q1
        )
        e_ref[tile(i)] = to_e
        w_ref[tile(i)] = to_w

    hc_ref[...] = jnp.zeros((7 * LEV, 8, 128), F32)
    hq_ref[...] = jnp.zeros((5 * MEM, 8, 128), F32)
    for lev in range(LEV):
        base = 24 + 12 * lev
        low = os[lev, 7:8] * os[lev, 8:9]
        high = os[lev, 263:264] * os[lev, 264:265]
        for n, (ref, slot) in enumerate(((un, 0), (kn, 3))):
            lower = jnp.where(northern, nh[base + slot + 2 : base + slot + 3], ref[lev, 263:264] * high)
            hc_ref[7 * lev + n, 0:2] = sh[base + slot : base + slot + 2]
            hc_ref[7 * lev + n, 2:3] = lower
            hc_ref[7 * lev + n, 3:4] = nh[base + slot : base + slot + 1]
            hc_ref[7 * lev + 2 + n, 0:1] = sh[base + slot + 1 : base + slot + 2]
            hc_ref[7 * lev + 2 + n, 1:2] = ref[lev, 7:8] * low
            hc_ref[7 * lev + 2 + n, 2:4] = nh[base + slot : base + slot + 2]
        for n in range(3):
            hc_ref[7 * lev + 4 + n, 0:2] = sh[base + 6 + 2 * n : base + 8 + 2 * n]
            hc_ref[7 * lev + 4 + n, 2:4] = nh[base + 6 + 2 * n : base + 8 + 2 * n]
    for m in range(MEM):
        for k in range(5):
            hq_ref[6 * k + m, 0:2] = q0[m, 4 + k : 6 + k]
            hq_ref[6 * k + m, 2:4] = q0[m, 262 + k : 264 + k]
    to_e = jnp.zeros((8, 128), F32)
    to_w = jnp.zeros((8, 128), F32)
    for m in range(MEM):
        q = hq_ref[12 + m]
        to_e = place(to_e, q, 126, 4 * m, 2, lane)
        to_w = place(to_w, q, 0, 4 * m + 2, 2, lane)
    for lev in range(LEV):
        u, k, ocean = hc_ref[7 * lev + 4], hc_ref[7 * lev + 5], hc_ref[7 * lev + 6]
        for x, spot in ((u, 32), (k, 35), (ocean, 38)):
            to_e = place(to_e, x, 127, spot + lev, 1, lane)
            to_w = place(to_w, x, 0 if spot == 38 else 127, spot + lev, 1, lane)
    e_ref[64:72] = to_e
    w_ref[64:72] = to_w


def last_kernel(wt, hc_ref, hq_ref, re_ref, rw_ref, q1_, out_ref, q1, new_ref, sems):
    lane = lanes()
    row = lax.broadcasted_iota(jnp.int32, (8, 128), 0)
    northern = lax.axis_index("lat") == lax.axis_size("lat") - 1
    folded = (row >= 2) & northern
    from_w, from_e = re_ref[64:72], rw_ref[64:72]
    both = jnp.where((lane & 2) == 0, from_w, from_e)
    for lev in range(LEV):
        ulo, klo, uup, kup, u, k, ocean = (hc_ref[7 * lev + n] for n in range(7))
        ocean_w = roll(from_w, -(38 + lev))
        ocean_e = roll(from_e, 127 - 38 - lev)

        def ends(x, spot, ocean=ocean, ocean_w=ocean_w, ocean_e=ocean_e):
            east = jnp.where(folded, roll(from_e, 127 - spot) * ocean, x * ocean_e)
            west = jnp.where(folded, roll(x, 1) * ocean_w, roll(from_w, -spot) * ocean)
            return jnp.where(lane == 127, east, x), jnp.where(lane == 0, west, roll(x, 1))

        ue, uw = ends(u, 32 + lev)
        ke, kw = ends(k, 35 + lev)
        w = weigh(ocean, (ue * TWELFTH, ke), (uw * TWELFTH, kw), (uup * TWELFTH, kup), (ulo * TWELFTH, klo))
        for t in range(2):
            m = 3 * t + lev
            q = [hq_ref[6 * n + m] for n in range(5)]
            new = apply(w, q[2], roll(both, 126 - 4 * m), q[0], q[1], q[3], q[4], lane)
            q1[m, 6:8] = new[0:2]
            q1[m, 264:266] = new[2:4]

    def body(i, carry):
        both = jnp.where((lane & 2) == 0, re_ref[tile(i)], rw_ref[tile(i)])
        for g in range(GROUPS):
            blk = chunk(i, 8 * g)

            def near(k, g=g):
                return chunk(i, 8 * g + 8 + k)

            for lev in range(LEV):
                w = [wt[9 * lev + n, blk] for n in range(9)]
                for t in range(2):
                    m = 3 * t + lev
                    sides = roll(both, 126 - 32 * g - 4 * m)
                    new_ref[t, lev, blk] = apply(
                        w, q1[m, near(0)], sides, q1[m, near(-2)], q1[m, near(-1)], q1[m, near(1)], q1[m, near(2)], lane
                    )
        return carry

    parts = []
    for n in range(4):
        lax.fori_loop(2 * n, 2 * n + 2, body, 0)
        rows = pl.ds(64 * n, 64)
        part = pltpu.make_async_copy(new_ref.at[:, :, rows], out_ref.at[:, :, rows], sems.at[n])
        part.start()
        parts.append(part)
    for part in parts:
        part.wait()


VMEM = pl.BlockSpec(memory_space=pltpu.VMEM)
HBM = pl.BlockSpec(memory_space=pltpu.HBM)


def call(kernel, name, operands, shapes, scratch=(), inside=VMEM, outside=None, alias=None):
    return pl.pallas_call(
        kernel,
        out_shape=[jax.ShapeDtypeStruct(s, F32) for s in shapes],
        in_specs=[inside] * len(operands),
        out_specs=outside or [VMEM] * len(shapes),
        scratch_shapes=list(scratch),
        input_output_aliases=alias or {},
        compiler_params=pltpu.CompilerParams(vmem_limit_bytes=16 * 2**20),
        name=name,
    )(*operands)


def patterns(height, width):
    def flat(make):
        return [
            (lat * width + lon, (to[0] % height) * width + to[1] % width)
            for lat in range(height)
            for lon in range(width)
            for to in [make(lat, lon)]
        ]

    def odd(pivot):
        def make(lat, lon):
            if lat == height - 1:
                return lat, pivot - 1 - lon
            if lat == 0:
                return lat, lon
            return (lat + 1, lon) if lat % 2 else (lat - 1, lon)

        return flat(make)

    east = flat(lambda lat, lon: (lat, lon + 1))
    west = flat(lambda lat, lon: (lat, lon - 1))
    pairs = flat(lambda lat, lon: (lat + 1, lon) if lat % 2 == 0 else (lat - 1, lon))
    return east, west, pairs, odd


def local(height, width, tracers, east_courant, north_courant, east_kappa, north_kappa, ocean_mask, fold_map):
    east, west, pairs, odd = patterns(height, width)
    fields = (tracers, east_courant, north_courant, east_kappa, north_kappa, ocean_mask)
    pivot = ((fold_map[0] + 1) // 128 + lax.axis_index("lon")) % width
    edge, side = (64, 128), (72, 128)
    ext, own, state = (LEV, ROWS + 16, 128), (LEV, ROWS, 128), (MEM, ROWS + 16, 128)
    a, b, e, w, q0, os, un, kn, ue, ke = call(
        pack_kernel,
        "pack",
        [pltpu.with_memory_space_constraint(x, pltpu.HBM) for x in fields],
        [edge] * 4 + [state, ext, ext, ext, own, own],
        [
            pltpu.VMEM((2, LEV, ROWS, 128), F32),
            pltpu.VMEM((LEV, ROWS, 128), jnp.int32),
            pltpu.VMEM(edge, F32),
            pltpu.VMEM(edge, F32),
            pltpu.SemaphoreType.DMA((6,)),
        ],
        inside=HBM,
    )
    weights = (9 * LEV, ROWS, 128)

    re = lax.ppermute(e, BOTH, east)
    rw = lax.ppermute(w, BOTH, west)
    ra = lax.ppermute(a, BOTH, pairs)
    rb = lax.switch(pivot, [lambda x, p=p: lax.ppermute(x, BOTH, odd(p)) for p in range(width)], b)
    wt, q1, e, w = call(inner_kernel, "inner", (q0, os, un, kn, ue, ke, re, rw), [weights, state, side, side])
    q0, os, un, kn, wt, q1, e, w, hc, hq = call(
        edge_kernel,
        "edge",
        (ue, ke, re, rw, ra, rb, q0, os, un, kn, wt, q1, e, w),
        [state, ext, ext, ext, weights, state, side, side, (7 * LEV, 8, 128), (5 * MEM, 8, 128)],
        [pltpu.VMEM(edge, F32), pltpu.VMEM(edge, F32)],
        alias={6 + n: n for n in range(8)},
    )
    re = lax.ppermute(e, BOTH, east)
    rw = lax.ppermute(w, BOTH, west)
    out, _ = call(
        last_kernel,
        "last",
        (wt, hc, hq, re, rw, q1),
        [(2, LEV, ROWS, 128), state],
        [pltpu.VMEM((2, LEV, ROWS, 128), F32), pltpu.SemaphoreType.DMA((4,))],
        outside=[HBM, VMEM],
        alias={5: 1},
    )
    return out


def solution(mesh):
    plane = P(None, "lat", "lon")
    grid = P(None, None, "lat", "lon")
    return jax.shard_map(
        functools.partial(local, mesh.shape["lat"], mesh.shape["lon"]),
        mesh=mesh,
        in_specs=(grid, plane, plane, plane, plane, plane, P("lon")),
        out_specs=grid,
        check_vma=False,
    )
```

```python
import functools

import jax
import jax.numpy as jnp
from jax import lax
from jax.experimental import pallas as pl
from jax.experimental.pallas import tpu as pltpu
from jax.sharding import PartitionSpec as P

BOTH = ("lat", "lon")
LEV = 3
MEM = 6
ROWS = 256
BLOCKS = 8
GROUPS = 4
TWELFTH = 1.0 / 12.0
F32 = jnp.float32


def lanes():
    return lax.broadcasted_iota(jnp.int32, (8, 128), 1)


def roll(x, shift):
    shift = shift % 128
    return x if shift == 0 else pltpu.roll(x, shift, axis=1)


def face(courant, kappa):
    size = jnp.abs(courant)
    slope = 3.0 * size + kappa
    seven = 7.0 * courant
    return -(courant + size), seven + slope, seven - slope, size - courant


def weigh(ocean, east, west, north, south):
    ea, eb, ec, ed = face(*east)
    wa, wb, wc, wd = face(*west)
    na, nb, nc, nd = face(*north)
    sa, sb, sc, sd = face(*south)
    return (
        ocean + ((wc - eb) + (sc - nb)),
        wa,
        wb - ea,
        wd - ec,
        -ed,
        sa,
        sb - na,
        sd - nc,
        -nd,
    )


def apply(w, q, sides, below2, below1, above1, above2, lane):
    west2 = roll(jnp.where(lane >= 126, sides, q), 2)
    west1 = roll(jnp.where(lane == 127, sides, q), 1)
    east1 = roll(jnp.where(lane == 0, sides, q), -1)
    east2 = roll(jnp.where(lane < 2, sides, q), -2)
    across = (w[1] * west2 + w[2] * west1) + (w[3] * east1 + w[4] * east2)
    along = (w[5] * below2 + w[6] * below1) + (w[7] * above1 + w[8] * above2)
    return w[0] * q + (across + along)


def place(kept, x, source, target, count, lane):
    moved = roll(x, target - source)
    if count == 1:
        here = lane == target
    else:
        here = (lane >= target) & (lane < target + count)
    return jnp.where(here, moved, kept)


def chunk(i, k=0):
    if isinstance(i, int):
        return pl.ds(32 * i + k, 8)
    return pl.ds(pl.multiple_of(32 * i, 32) + k, 8)


def tile(i):
    return pl.ds(8 * i, 8) if isinstance(i, int) else pl.ds(pl.multiple_of(8 * i, 8), 8)


def pack_kernel(
    t_in, ue_in, un_in, ke_in, kn_in, m_in,
    a_ref, b_ref, e_ref, w_ref, q0, os, un, kn, ue, ke,
    tv, mv, nb, sb, sems,
):
    half = ROWS // 2
    copies = []
    for n in range(2):
        rows = pl.ds(half * n, half)
        for source, target in (
            (m_in.at[:, rows], mv.at[:, rows]),
            (t_in.at[:, :, rows], tv.at[:, :, rows]),
            (ue_in.at[:, rows], ue.at[:, rows]),
            (ke_in.at[:, rows], ke.at[:, rows]),
        ):
            copies.append(pltpu.make_async_copy(source, target, sems.at[len(copies)]))
    own = pl.ds(8, ROWS)
    copies.append(pltpu.make_async_copy(un_in, un.at[:, own], sems.at[8]))
    copies.append(pltpu.make_async_copy(kn_in, kn.at[:, own], sems.at[9]))
    for c in copies:
        c.start()
    lane = lanes()
    nb[...] = jnp.zeros((64, 128), F32)
    sb[...] = jnp.zeros((64, 128), F32)

    def body(i, carry):
        to_e = jnp.zeros((8, 128), F32)
        to_w = jnp.zeros((8, 128), F32)
        both = jnp.zeros((8, 128), F32)
        for g in range(GROUPS):
            blk, ext = chunk(i, 8 * g), chunk(i, 8 * g + 8)
            for lev in range(LEV):
                ocean = mv[lev, blk].astype(F32)
                os[lev, ext] = ocean
                at = 32 * g + 24 + lev
                to_e = place(to_e, ue[lev, blk] * ocean, 127, at, 1, lane)
                to_e = place(to_e, ke[lev, blk] * ocean, 127, at + 3, 1, lane)
                to_w = place(to_w, ocean, 0, at, 1, lane)
                for t in range(2):
                    m = 3 * t + lev
                    q = tv[t, lev, blk] * ocean
                    q0[m, ext] = q
                    both = place(both, q, 126, 32 * g + 4 * m, 4, lane)
        states = (lane & 31) < 24
        e_ref[tile(i)] = jnp.where(states, both, to_e)
        w_ref[tile(i)] = jnp.where(states, both, to_w)
        return carry

    for n in range(2):
        for c in copies[4 * n : 4 * n + 4]:
            c.wait()
        lax.fori_loop(BLOCKS // 2 * n, BLOCKS // 2 * (n + 1), body, 0)
    for c in copies[8:]:
        c.wait()
    for lev in range(LEV):
        base = 24 + 12 * lev
        for out, lo, rows, faces in ((nb, ROWS - 8, slice(6, 8), slice(5, 7)), (sb, 0, slice(0, 2), slice(0, 2))):
            blk, ext = pl.ds(lo, 8), pl.ds(lo + 8, 8)
            ocean = os[lev, ext]
            beside = jnp.where(lane == 127, 1.0, roll(ocean, -1))
            up = slice(faces.start + 1, faces.stop + 1)
            shut = ocean[faces] * ocean[up]
            u, k = un[lev, ext], kn[lev, ext]
            out[base : base + 2] = u[faces] * shut
            out[base + 3 : base + 5] = k[faces] * shut
            if lo:
                out[base + 2 : base + 3] = u[7:8] * ocean[7:8]
                out[base + 5 : base + 6] = k[7:8] * ocean[7:8]
            open_e = ocean * beside
            out[base + 6 : base + 8] = (ue[lev, blk] * open_e)[rows]
            out[base + 8 : base + 10] = (ke[lev, blk] * open_e)[rows]
            out[base + 10 : base + 12] = ocean[rows]
            for t in range(2):
                m = 3 * t + lev
                q = q0[m, ext]
                out[4 * m : 4 * m + 4] = q[4:8] if lo else q[0:4]
    even = lax.rem(lax.axis_index("lat"), 2) == 0
    north, south = nb[...], sb[...]
    a_ref[...] = jnp.where(even, north, south)
    b_ref[...] = jnp.where(even, south, north)


def flip(x):
    return jnp.take_along_axis(x, 127 - lax.broadcasted_iota(jnp.int32, x.shape, 1), axis=1)


def step_kernel(
    ue, ke, re_ref, rw_ref, ra_ref, rb_ref, q0_, os_, un_, kn_,
    q0, os, un, kn, wt, q1, s_ref, hc_ref, hq_ref,
    nh, sh,
):
    lane = lanes()
    lat = lax.axis_index("lat")
    even = lax.rem(lat, 2) == 0
    southern = lat == 0
    northern = lat == lax.axis_size("lat") - 1
    first, second = ra_ref[...], rb_ref[...]
    sh[...] = jnp.where(southern, 0.0, jnp.where(even, second, first))
    nh[...] = jnp.where(even, first, second)

    @pl.when(northern)
    def _():
        f = flip(rb_ref[...])
        shifted = roll(f, -1)
        for m in range(MEM):
            for r in range(4):
                nh[4 * m + r : 4 * m + r + 1] = f[4 * m + 3 - r : 4 * m + 4 - r]
        for lev in range(LEV):
            base = 24 + 12 * lev
            for to, source, x in (
                (0, 1, -f), (1, 0, -f), (2, 2, -f), (3, 4, f), (4, 3, f), (5, 5, f),
                (6, 7, -shifted), (7, 6, -shifted), (8, 9, shifted), (9, 8, shifted), (10, 11, f), (11, 10, f),
            ):
                nh[base + to : base + to + 1] = x[base + source : base + source + 1]

    for m in range(MEM):
        q0[m, 4:8] = sh[4 * m : 4 * m + 4]
        q0[m, 264:268] = nh[4 * m : 4 * m + 4]
    for lev in range(LEV):
        base = 24 + 12 * lev
        top = os[lev, 263:264]
        os[lev, 264:265] = jnp.where(northern, top, nh[base + 10 : base + 11])
        os[lev, 7:8] = sh[base + 11 : base + 12]
        un[lev, 7:8] = sh[base + 2 : base + 3]
        kn[lev, 7:8] = sh[base + 5 : base + 6]

    def weights(i, carry):
        from_w, from_e = re_ref[tile(i)], rw_ref[tile(i)]
        for g in range(GROUPS):
            blk = chunk(i, 8 * g)

            def near(k, g=g):
                return chunk(i, 8 * g + 8 + k)

            for lev in range(LEV):
                ocean = os[lev, near(0)]
                spot = 32 * g + 24 + lev
                beside = jnp.where(lane == 127, roll(from_e, 127 - spot), roll(ocean, -1))
                shut = ocean * beside
                u = ue[lev, blk] * (shut * TWELFTH)
                k = ke[lev, blk] * shut
                uw = jnp.where(lane == 0, roll(from_w, -spot) * (ocean * TWELFTH), roll(u, 1))
                kw = jnp.where(lane == 0, roll(from_w, -(spot + 3)) * ocean, roll(k, 1))
                shut = ocean * os[lev, near(1)]
                north = un[lev, near(0)] * (shut * TWELFTH), kn[lev, near(0)] * shut
                shut = ocean * os[lev, near(-1)]
                south = un[lev, near(-1)] * (shut * TWELFTH), kn[lev, near(-1)] * shut
                w = weigh(ocean, (u, k), (uw, kw), north, south)
                for n in range(9):
                    wt[9 * lev + n, blk] = w[n]
        return carry

    lax.fori_loop(0, BLOCKS, weights, 0)

    def update(i, carry):
        both = jnp.where((lane & 2) == 0, re_ref[tile(i)], rw_ref[tile(i)])
        strip = jnp.zeros((8, 128), F32)
        for g in range(GROUPS):
            blk = chunk(i, 8 * g)

            def near(k, g=g):
                return chunk(i, 8 * g + 8 + k)

            for lev in range(LEV):
                w = [wt[9 * lev + n, blk] for n in range(9)]
                for t in range(2):
                    m = 3 * t + lev
                    spot = 32 * g + 4 * m
                    sides = roll(both, 126 - spot)
                    new = apply(
                        w, q0[m, near(0)], sides, q0[m, near(-2)], q0[m, near(-1)], q0[m, near(1)], q0[m, near(2)], lane
                    )
                    q1[m, near(0)] = new
                    strip = place(strip, new, 126, spot, 4, lane)
        s_ref[tile(i)] = strip
        return carry

    lax.fori_loop(0, BLOCKS, update, 0)

    hc_ref[...] = jnp.zeros((7 * LEV, 8, 128), F32)
    hq_ref[...] = jnp.zeros((5 * MEM, 8, 128), F32)
    for lev in range(LEV):
        base = 24 + 12 * lev
        low = os[lev, 7:8] * os[lev, 8:9]
        high = os[lev, 263:264] * os[lev, 264:265]
        for n, (ref, slot) in enumerate(((un, 0), (kn, 3))):
            lower = jnp.where(northern, nh[base + slot + 2 : base + slot + 3], ref[lev, 263:264] * high)
            hc_ref[7 * lev + n, 0:2] = sh[base + slot : base + slot + 2]
            hc_ref[7 * lev + n, 2:3] = lower
            hc_ref[7 * lev + n, 3:4] = nh[base + slot : base + slot + 1]
            hc_ref[7 * lev + 2 + n, 0:1] = sh[base + slot + 1 : base + slot + 2]
            hc_ref[7 * lev + 2 + n, 1:2] = ref[lev, 7:8] * low
            hc_ref[7 * lev + 2 + n, 2:4] = nh[base + slot : base + slot + 2]
        for n in range(3):
            hc_ref[7 * lev + 4 + n, 0:2] = sh[base + 6 + 2 * n : base + 8 + 2 * n]
            hc_ref[7 * lev + 4 + n, 2:4] = nh[base + 6 + 2 * n : base + 8 + 2 * n]
    for m in range(MEM):
        for k in range(5):
            hq_ref[6 * k + m, 0:2] = q0[m, 4 + k : 6 + k]
            hq_ref[6 * k + m, 2:4] = q0[m, 262 + k : 264 + k]
    strip = jnp.zeros((8, 128), F32)
    for m in range(MEM):
        strip = place(strip, hq_ref[12 + m], 126, 4 * m, 4, lane)
    for lev in range(LEV):
        u, k, ocean = hc_ref[7 * lev + 4], hc_ref[7 * lev + 5], hc_ref[7 * lev + 6]
        strip = place(strip, u, 127, 32 + lev, 1, lane)
        strip = place(strip, k, 127, 35 + lev, 1, lane)
        strip = place(strip, ocean, 127, 38 + 2 * lev, 2, lane)
    s_ref[64:72] = strip


def last_kernel(wt, hc_ref, hq_ref, re_ref, rw_ref, q1_, out_ref, q1, new_ref, sems):
    lane = lanes()
    row = lax.broadcasted_iota(jnp.int32, (8, 128), 0)
    northern = lax.axis_index("lat") == lax.axis_size("lat") - 1
    folded = (row >= 2) & northern
    from_w, from_e = re_ref[64:72], rw_ref[64:72]
    both = jnp.where((lane & 2) == 0, from_w, from_e)
    for lev in range(LEV):
        ulo, klo, uup, kup, u, k, ocean = (hc_ref[7 * lev + n] for n in range(7))
        ocean_w = roll(from_w, -(38 + 2 * lev))
        ocean_e = roll(from_e, 127 - 39 - 2 * lev)

        def ends(x, spot, ocean=ocean, ocean_w=ocean_w, ocean_e=ocean_e):
            east = jnp.where(folded, roll(from_e, 127 - spot) * ocean, x * ocean_e)
            west = jnp.where(folded, roll(x, 1) * ocean_w, roll(from_w, -spot) * ocean)
            return jnp.where(lane == 127, east, x), jnp.where(lane == 0, west, roll(x, 1))

        ue, uw = ends(u, 32 + lev)
        ke, kw = ends(k, 35 + lev)
        w = weigh(ocean, (ue * TWELFTH, ke), (uw * TWELFTH, kw), (uup * TWELFTH, kup), (ulo * TWELFTH, klo))
        for t in range(2):
            m = 3 * t + lev
            q = [hq_ref[6 * n + m] for n in range(5)]
            new = apply(w, q[2], roll(both, 126 - 4 * m), q[0], q[1], q[3], q[4], lane)
            q1[m, 6:8] = new[0:2]
            q1[m, 264:266] = new[2:4]

    def body(i, carry):
        both = jnp.where((lane & 2) == 0, re_ref[tile(i)], rw_ref[tile(i)])
        for g in range(GROUPS):
            blk = chunk(i, 8 * g)

            def near(k, g=g):
                return chunk(i, 8 * g + 8 + k)

            for lev in range(LEV):
                w = [wt[9 * lev + n, blk] for n in range(9)]
                for t in range(2):
                    m = 3 * t + lev
                    sides = roll(both, 126 - 32 * g - 4 * m)
                    new_ref[t, lev, blk] = apply(
                        w, q1[m, near(0)], sides, q1[m, near(-2)], q1[m, near(-1)], q1[m, near(1)], q1[m, near(2)], lane
                    )
        return carry

    parts = []
    for n in range(4):
        lax.fori_loop(2 * n, 2 * n + 2, body, 0)
        rows = pl.ds(64 * n, 64)
        part = pltpu.make_async_copy(new_ref.at[:, :, rows], out_ref.at[:, :, rows], sems.at[n])
        part.start()
        parts.append(part)
    for part in parts:
        part.wait()


VMEM = pl.BlockSpec(memory_space=pltpu.VMEM)
HBM = pl.BlockSpec(memory_space=pltpu.HBM)


def call(kernel, name, operands, shapes, scratch=(), inside=VMEM, outside=None, alias=None):
    return pl.pallas_call(
        kernel,
        out_shape=[jax.ShapeDtypeStruct(s, F32) for s in shapes],
        in_specs=[inside] * len(operands),
        out_specs=outside or [VMEM] * len(shapes),
        scratch_shapes=list(scratch),
        input_output_aliases=alias or {},
        compiler_params=pltpu.CompilerParams(vmem_limit_bytes=16 * 2**20),
        name=name,
    )(*operands)


def patterns(height, width):
    def flat(make):
        return [
            (lat * width + lon, (to[0] % height) * width + to[1] % width)
            for lat in range(height)
            for lon in range(width)
            for to in [make(lat, lon)]
        ]

    def odd(pivot):
        def make(lat, lon):
            if lat == height - 1:
                return lat, pivot - 1 - lon
            if lat == 0:
                return lat, lon
            return (lat + 1, lon) if lat % 2 else (lat - 1, lon)

        return flat(make)

    east = flat(lambda lat, lon: (lat, lon + 1))
    west = flat(lambda lat, lon: (lat, lon - 1))
    pairs = flat(lambda lat, lon: (lat + 1, lon) if lat % 2 == 0 else (lat - 1, lon))
    return east, west, pairs, odd


def local(height, width, tracers, east_courant, north_courant, east_kappa, north_kappa, ocean_mask, fold_map):
    east, west, pairs, odd = patterns(height, width)
    fields = (tracers, east_courant, north_courant, east_kappa, north_kappa, ocean_mask)
    pivot = ((fold_map[0] + 1) // 128 + lax.axis_index("lon")) % width
    edge, side = (64, 128), (72, 128)
    ext, own, state = (LEV, ROWS + 16, 128), (LEV, ROWS, 128), (MEM, ROWS + 16, 128)
    a, b, e, w, q0, os, un, kn, ue, ke = call(
        pack_kernel,
        "pack",
        [pltpu.with_memory_space_constraint(x, pltpu.HBM) for x in fields],
        [edge] * 4 + [state, ext, ext, ext, own, own],
        [
            pltpu.VMEM((2, LEV, ROWS, 128), F32),
            pltpu.VMEM((LEV, ROWS, 128), jnp.int32),
            pltpu.VMEM(edge, F32),
            pltpu.VMEM(edge, F32),
            pltpu.SemaphoreType.DMA((10,)),
        ],
        inside=HBM,
    )
    weights = (9 * LEV, ROWS, 128)

    re = lax.ppermute(e, BOTH, east)
    rw = lax.ppermute(w, BOTH, west)
    ra = lax.ppermute(a, BOTH, pairs)
    rb = lax.switch(pivot, [lambda x, p=p: lax.ppermute(x, BOTH, odd(p)) for p in range(width)], b)
    q0, os, un, kn, wt, q1, s, hc, hq = call(
        step_kernel,
        "step",
        (ue, ke, re, rw, ra, rb, q0, os, un, kn),
        [state, ext, ext, ext, weights, state, side, (7 * LEV, 8, 128), (5 * MEM, 8, 128)],
        [pltpu.VMEM(edge, F32), pltpu.VMEM(edge, F32)],
        alias={6 + n: n for n in range(4)},
    )
    re = lax.ppermute(s, BOTH, east)
    rw = lax.ppermute(s, BOTH, west)
    out, _ = call(
        last_kernel,
        "last",
        (wt, hc, hq, re, rw, q1),
        [(2, LEV, ROWS, 128), state],
        [pltpu.VMEM((2, LEV, ROWS, 128), F32), pltpu.SemaphoreType.DMA((4,))],
        outside=[HBM, VMEM],
        alias={5: 1},
    )
    return out


def solution(mesh):
    plane = P(None, "lat", "lon")
    grid = P(None, None, "lat", "lon")
    return jax.shard_map(
        functools.partial(local, mesh.shape["lat"], mesh.shape["lon"]),
        mesh=mesh,
        in_specs=(grid, plane, plane, plane, plane, plane, P("lon")),
        out_specs=grid,
        check_vma=False,
    )
```

```python
import functools

import jax
import jax.numpy as jnp
from jax import lax
from jax.experimental import pallas as pl
from jax.experimental.pallas import tpu as pltpu
from jax.sharding import PartitionSpec as P

BOTH = ("lat", "lon")
LEV = 3
MEM = 6
ROWS = 256
BLOCKS = 8
GROUPS = 4
TWELFTH = 1.0 / 12.0
F32 = jnp.float32


def lanes():
    return lax.broadcasted_iota(jnp.int32, (8, 128), 1)


def roll(x, shift):
    shift = shift % 128
    return x if shift == 0 else pltpu.roll(x, shift, axis=1)


def face(courant, kappa):
    size = jnp.abs(courant)
    slope = 3.0 * size + kappa
    seven = 7.0 * courant
    return -(courant + size), seven + slope, seven - slope, size - courant


def weigh(ocean, east, west, north, south):
    ea, eb, ec, ed = face(*east)
    wa, wb, wc, wd = face(*west)
    na, nb, nc, nd = face(*north)
    sa, sb, sc, sd = face(*south)
    return (
        ocean + ((wc - eb) + (sc - nb)),
        wa,
        wb - ea,
        wd - ec,
        -ed,
        sa,
        sb - na,
        sd - nc,
        -nd,
    )


def apply(w, q, sides, below2, below1, above1, above2, lane):
    west2 = roll(jnp.where(lane >= 126, sides, q), 2)
    west1 = roll(jnp.where(lane == 127, sides, q), 1)
    east1 = roll(jnp.where(lane == 0, sides, q), -1)
    east2 = roll(jnp.where(lane < 2, sides, q), -2)
    across = (w[1] * west2 + w[2] * west1) + (w[3] * east1 + w[4] * east2)
    along = (w[5] * below2 + w[6] * below1) + (w[7] * above1 + w[8] * above2)
    return w[0] * q + (across + along)


def place(kept, x, source, target, count, lane):
    moved = roll(x, target - source)
    if count == 1:
        here = lane == target
    else:
        here = (lane >= target) & (lane < target + count)
    return jnp.where(here, moved, kept)


def chunk(i, k=0):
    if isinstance(i, int):
        return pl.ds(32 * i + k, 8)
    return pl.ds(pl.multiple_of(32 * i, 32) + k, 8)


def tile(i):
    return pl.ds(8 * i, 8) if isinstance(i, int) else pl.ds(pl.multiple_of(8 * i, 8), 8)


def pack_kernel(
    t_in, ue_in, un_in, ke_in, kn_in, m_in,
    b_ref, e_ref, w_ref, a_ref, f_ref, q0, os, un, kn, ue, ke,
    tv, mv, nb, sb, sems,
):
    half = ROWS // 2
    copies = []
    for n in range(2):
        rows = pl.ds(half * n, half)
        for source, target in (
            (m_in.at[:, rows], mv.at[:, rows]),
            (t_in.at[:, :, rows], tv.at[:, :, rows]),
            (ue_in.at[:, rows], ue.at[:, rows]),
            (ke_in.at[:, rows], ke.at[:, rows]),
        ):
            copies.append(pltpu.make_async_copy(source, target, sems.at[len(copies)]))
    own = pl.ds(8, ROWS)
    copies.append(pltpu.make_async_copy(un_in, un.at[:, own], sems.at[8]))
    copies.append(pltpu.make_async_copy(kn_in, kn.at[:, own], sems.at[9]))
    for c in copies:
        c.start()
    lane = lanes()
    nb[...] = jnp.zeros((64, 128), F32)
    sb[...] = jnp.zeros((64, 128), F32)

    def body(i, carry):
        to_e = jnp.zeros((8, 128), F32)
        to_w = jnp.zeros((8, 128), F32)
        both = jnp.zeros((8, 128), F32)
        for g in range(GROUPS):
            blk, ext = chunk(i, 8 * g), chunk(i, 8 * g + 8)
            for lev in range(LEV):
                ocean = mv[lev, blk].astype(F32)
                os[lev, ext] = ocean
                at = 32 * g + 24 + lev
                to_e = place(to_e, ue[lev, blk] * ocean, 127, at, 1, lane)
                to_e = place(to_e, ke[lev, blk] * ocean, 127, at + 3, 1, lane)
                to_w = place(to_w, ocean, 0, at, 1, lane)
                for t in range(2):
                    m = 3 * t + lev
                    q = tv[t, lev, blk] * ocean
                    q0[m, ext] = q
                    both = place(both, q, 126, 32 * g + 4 * m, 4, lane)
        states = (lane & 31) < 24
        e_ref[tile(i)] = jnp.where(states, both, to_e)
        w_ref[tile(i)] = jnp.where(states, both, to_w)
        return carry

    for n in range(2):
        for c in copies[4 * n : 4 * n + 4]:
            c.wait()
        lax.fori_loop(BLOCKS // 2 * n, BLOCKS // 2 * (n + 1), body, 0)
    for c in copies[8:]:
        c.wait()
    for lev in range(LEV):
        base = 24 + 12 * lev
        for out, lo, rows, faces in ((nb, ROWS - 8, slice(6, 8), slice(5, 7)), (sb, 0, slice(0, 2), slice(0, 2))):
            blk, ext = pl.ds(lo, 8), pl.ds(lo + 8, 8)
            ocean = os[lev, ext]
            beside = jnp.where(lane == 127, 1.0, roll(ocean, -1))
            up = slice(faces.start + 1, faces.stop + 1)
            shut = ocean[faces] * ocean[up]
            u, k = un[lev, ext], kn[lev, ext]
            out[base : base + 2] = u[faces] * shut
            out[base + 3 : base + 5] = k[faces] * shut
            if lo:
                out[base + 2 : base + 3] = u[7:8] * ocean[7:8]
                out[base + 5 : base + 6] = k[7:8] * ocean[7:8]
            open_e = ocean * beside
            out[base + 6 : base + 8] = (ue[lev, blk] * open_e)[rows]
            out[base + 8 : base + 10] = (ke[lev, blk] * open_e)[rows]
            out[base + 10 : base + 12] = ocean[rows]
            for t in range(2):
                m = 3 * t + lev
                q = q0[m, ext]
                out[4 * m : 4 * m + 4] = q[4:8] if lo else q[0:4]
    even = lax.rem(lax.axis_index("lat"), 2) == 0
    north, south = nb[...], sb[...]
    a_ref[...] = jnp.where(even, north, south)
    b_ref[...] = jnp.where(even, south, north)
    f_ref[...] = north


def flip(x):
    return jnp.take_along_axis(x, 127 - lax.broadcasted_iota(jnp.int32, x.shape, 1), axis=1)


def step_kernel(
    ra_ref, rb_ref, re_ref, rw_ref, rf_ref, ue, ke, q0_, os_, un_, kn_,
    q0, os, un, kn, wt, q1, s_ref, hc_ref, hq_ref,
    nh, sh,
):
    lane = lanes()
    lat = lax.axis_index("lat")
    even = lax.rem(lat, 2) == 0
    southern = lat == 0
    northern = lat == lax.axis_size("lat") - 1
    first, second = ra_ref[...], rb_ref[...]
    sh[...] = jnp.where(southern, 0.0, jnp.where(even, second, first))
    nh[...] = jnp.where(even, first, second)

    @pl.when(northern)
    def _():
        f = flip(rf_ref[...])
        shifted = roll(f, -1)
        for m in range(MEM):
            for r in range(4):
                nh[4 * m + r : 4 * m + r + 1] = f[4 * m + 3 - r : 4 * m + 4 - r]
        for lev in range(LEV):
            base = 24 + 12 * lev
            for to, source, x in (
                (0, 1, -f), (1, 0, -f), (2, 2, -f), (3, 4, f), (4, 3, f), (5, 5, f),
                (6, 7, -shifted), (7, 6, -shifted), (8, 9, shifted), (9, 8, shifted), (10, 11, f), (11, 10, f),
            ):
                nh[base + to : base + to + 1] = x[base + source : base + source + 1]

    for m in range(MEM):
        q0[m, 4:8] = sh[4 * m : 4 * m + 4]
        q0[m, 264:268] = nh[4 * m : 4 * m + 4]
    for lev in range(LEV):
        base = 24 + 12 * lev
        top = os[lev, 263:264]
        os[lev, 264:265] = jnp.where(northern, top, nh[base + 10 : base + 11])
        os[lev, 7:8] = sh[base + 11 : base + 12]
        un[lev, 7:8] = sh[base + 2 : base + 3]
        kn[lev, 7:8] = sh[base + 5 : base + 6]

    def weights(i, carry):
        from_w, from_e = re_ref[tile(i)], rw_ref[tile(i)]
        for g in range(GROUPS):
            blk = chunk(i, 8 * g)

            def near(k, g=g):
                return chunk(i, 8 * g + 8 + k)

            for lev in range(LEV):
                ocean = os[lev, near(0)]
                spot = 32 * g + 24 + lev
                beside = jnp.where(lane == 127, roll(from_e, 127 - spot), roll(ocean, -1))
                shut = ocean * beside
                u = ue[lev, blk] * (shut * TWELFTH)
                k = ke[lev, blk] * shut
                uw = jnp.where(lane == 0, roll(from_w, -spot) * (ocean * TWELFTH), roll(u, 1))
                kw = jnp.where(lane == 0, roll(from_w, -(spot + 3)) * ocean, roll(k, 1))
                shut = ocean * os[lev, near(1)]
                north = un[lev, near(0)] * (shut * TWELFTH), kn[lev, near(0)] * shut
                shut = ocean * os[lev, near(-1)]
                south = un[lev, near(-1)] * (shut * TWELFTH), kn[lev, near(-1)] * shut
                w = weigh(ocean, (u, k), (uw, kw), north, south)
                for n in range(9):
                    wt[9 * lev + n, blk] = w[n]
        return carry

    lax.fori_loop(0, BLOCKS, weights, 0)

    def update(i, carry):
        both = jnp.where((lane & 2) == 0, re_ref[tile(i)], rw_ref[tile(i)])
        strip = jnp.zeros((8, 128), F32)
        for g in range(GROUPS):
            blk = chunk(i, 8 * g)

            def near(k, g=g):
                return chunk(i, 8 * g + 8 + k)

            for lev in range(LEV):
                w = [wt[9 * lev + n, blk] for n in range(9)]
                for t in range(2):
                    m = 3 * t + lev
                    spot = 32 * g + 4 * m
                    sides = roll(both, 126 - spot)
                    new = apply(
                        w, q0[m, near(0)], sides, q0[m, near(-2)], q0[m, near(-1)], q0[m, near(1)], q0[m, near(2)], lane
                    )
                    q1[m, near(0)] = new
                    strip = place(strip, new, 126, spot, 4, lane)
        s_ref[tile(i)] = strip
        return carry

    lax.fori_loop(0, BLOCKS, update, 0)

    hc_ref[...] = jnp.zeros((7 * LEV, 8, 128), F32)
    hq_ref[...] = jnp.zeros((5 * MEM, 8, 128), F32)
    for lev in range(LEV):
        base = 24 + 12 * lev
        low = os[lev, 7:8] * os[lev, 8:9]
        high = os[lev, 263:264] * os[lev, 264:265]
        for n, (ref, slot) in enumerate(((un, 0), (kn, 3))):
            lower = jnp.where(northern, nh[base + slot + 2 : base + slot + 3], ref[lev, 263:264] * high)
            hc_ref[7 * lev + n, 0:2] = sh[base + slot : base + slot + 2]
            hc_ref[7 * lev + n, 2:3] = lower
            hc_ref[7 * lev + n, 3:4] = nh[base + slot : base + slot + 1]
            hc_ref[7 * lev + 2 + n, 0:1] = sh[base + slot + 1 : base + slot + 2]
            hc_ref[7 * lev + 2 + n, 1:2] = ref[lev, 7:8] * low
            hc_ref[7 * lev + 2 + n, 2:4] = nh[base + slot : base + slot + 2]
        for n in range(3):
            hc_ref[7 * lev + 4 + n, 0:2] = sh[base + 6 + 2 * n : base + 8 + 2 * n]
            hc_ref[7 * lev + 4 + n, 2:4] = nh[base + 6 + 2 * n : base + 8 + 2 * n]
    for m in range(MEM):
        for k in range(5):
            hq_ref[6 * k + m, 0:2] = q0[m, 4 + k : 6 + k]
            hq_ref[6 * k + m, 2:4] = q0[m, 262 + k : 264 + k]
    strip = jnp.zeros((8, 128), F32)
    for m in range(MEM):
        strip = place(strip, hq_ref[12 + m], 126, 4 * m, 4, lane)
    for lev in range(LEV):
        u, k, ocean = hc_ref[7 * lev + 4], hc_ref[7 * lev + 5], hc_ref[7 * lev + 6]
        strip = place(strip, u, 127, 32 + lev, 1, lane)
        strip = place(strip, k, 127, 35 + lev, 1, lane)
        strip = place(strip, ocean, 127, 38 + 2 * lev, 2, lane)
    s_ref[64:72] = strip


def last_kernel(wt, hc_ref, hq_ref, rw_ref, re_ref, q1_, out_ref, q1, new_ref, sems):
    lane = lanes()
    row = lax.broadcasted_iota(jnp.int32, (8, 128), 0)
    northern = lax.axis_index("lat") == lax.axis_size("lat") - 1
    folded = (row >= 2) & northern
    from_w, from_e = re_ref[64:72], rw_ref[64:72]
    both = jnp.where((lane & 2) == 0, from_w, from_e)
    for lev in range(LEV):
        ulo, klo, uup, kup, u, k, ocean = (hc_ref[7 * lev + n] for n in range(7))
        ocean_w = roll(from_w, -(38 + 2 * lev))
        ocean_e = roll(from_e, 127 - 39 - 2 * lev)

        def ends(x, spot, ocean=ocean, ocean_w=ocean_w, ocean_e=ocean_e):
            east = jnp.where(folded, roll(from_e, 127 - spot) * ocean, x * ocean_e)
            west = jnp.where(folded, roll(x, 1) * ocean_w, roll(from_w, -spot) * ocean)
            return jnp.where(lane == 127, east, x), jnp.where(lane == 0, west, roll(x, 1))

        ue, uw = ends(u, 32 + lev)
        ke, kw = ends(k, 35 + lev)
        w = weigh(ocean, (ue * TWELFTH, ke), (uw * TWELFTH, kw), (uup * TWELFTH, kup), (ulo * TWELFTH, klo))
        for t in range(2):
            m = 3 * t + lev
            q = [hq_ref[6 * n + m] for n in range(5)]
            new = apply(w, q[2], roll(both, 126 - 4 * m), q[0], q[1], q[3], q[4], lane)
            q1[m, 6:8] = new[0:2]
            q1[m, 264:266] = new[2:4]

    def body(i, carry):
        both = jnp.where((lane & 2) == 0, re_ref[tile(i)], rw_ref[tile(i)])
        for g in range(GROUPS):
            blk = chunk(i, 8 * g)

            def near(k, g=g):
                return chunk(i, 8 * g + 8 + k)

            for lev in range(LEV):
                w = [wt[9 * lev + n, blk] for n in range(9)]
                for t in range(2):
                    m = 3 * t + lev
                    sides = roll(both, 126 - 32 * g - 4 * m)
                    new_ref[t, lev, blk] = apply(
                        w, q1[m, near(0)], sides, q1[m, near(-2)], q1[m, near(-1)], q1[m, near(1)], q1[m, near(2)], lane
                    )
        return carry

    parts = []
    for n in range(4):
        lax.fori_loop(2 * n, 2 * n + 2, body, 0)
        rows = pl.ds(64 * n, 64)
        part = pltpu.make_async_copy(new_ref.at[:, :, rows], out_ref.at[:, :, rows], sems.at[n])
        part.start()
        parts.append(part)
    for part in parts:
        part.wait()


VMEM = pl.BlockSpec(memory_space=pltpu.VMEM)
HBM = pl.BlockSpec(memory_space=pltpu.HBM)


def call(kernel, name, operands, shapes, scratch=(), inside=VMEM, outside=None, alias=None):
    return pl.pallas_call(
        kernel,
        out_shape=[jax.ShapeDtypeStruct(s, F32) for s in shapes],
        in_specs=[inside] * len(operands),
        out_specs=outside or [VMEM] * len(shapes),
        scratch_shapes=list(scratch),
        input_output_aliases=alias or {},
        compiler_params=pltpu.CompilerParams(vmem_limit_bytes=16 * 2**20),
        name=name,
    )(*operands)


def patterns(height, width):
    def flat(make):
        return [
            (lat * width + lon, (to[0] % height) * width + to[1] % width)
            for lat in range(height)
            for lon in range(width)
            for to in [make(lat, lon)]
        ]

    def odd(lat, lon):
        if lat in (0, height - 1):
            return lat, lon
        return (lat + 1, lon) if lat % 2 else (lat - 1, lon)

    def fold(pivot):
        top = (height - 1) * width
        return [(top + lon, top + (pivot - 1 - lon) % width) for lon in range(width)]

    east = flat(lambda lat, lon: (lat, lon + 1))
    west = flat(lambda lat, lon: (lat, lon - 1))
    pairs = flat(lambda lat, lon: (lat + 1, lon) if lat % 2 == 0 else (lat - 1, lon))
    return east, west, pairs, flat(odd), fold


def local(height, width, tracers, east_courant, north_courant, east_kappa, north_kappa, ocean_mask, fold_map):
    east, west, pairs, odd, fold = patterns(height, width)
    fields = (tracers, east_courant, north_courant, east_kappa, north_kappa, ocean_mask)
    pivot = ((fold_map[0] + 1) // 128 + lax.axis_index("lon")) % width
    edge, side = (64, 128), (72, 128)
    ext, own, state = (LEV, ROWS + 16, 128), (LEV, ROWS, 128), (MEM, ROWS + 16, 128)
    b, e, w, a, f, q0, os, un, kn, ue, ke = call(
        pack_kernel,
        "pack",
        [pltpu.with_memory_space_constraint(x, pltpu.HBM) for x in fields],
        [edge] * 5 + [state, ext, ext, ext, own, own],
        [
            pltpu.VMEM((2, LEV, ROWS, 128), F32),
            pltpu.VMEM((LEV, ROWS, 128), jnp.int32),
            pltpu.VMEM(edge, F32),
            pltpu.VMEM(edge, F32),
            pltpu.SemaphoreType.DMA((10,)),
        ],
        inside=HBM,
    )
    weights = (9 * LEV, ROWS, 128)

    rb = lax.ppermute(b, BOTH, odd)
    re = lax.ppermute(e, BOTH, east)
    rw = lax.ppermute(w, BOTH, west)
    ra = lax.ppermute(a, BOTH, pairs)
    rf = lax.switch(pivot, [lambda x, p=p: lax.ppermute(x, BOTH, fold(p)) for p in range(width)], f)
    q0, os, un, kn, wt, q1, s, hc, hq = call(
        step_kernel,
        "step",
        (ra, rb, re, rw, rf, ue, ke, q0, os, un, kn),
        [state, ext, ext, ext, weights, state, side, (7 * LEV, 8, 128), (5 * MEM, 8, 128)],
        [pltpu.VMEM(edge, F32), pltpu.VMEM(edge, F32)],
        alias={7 + n: n for n in range(4)},
    )
    re = lax.ppermute(s, BOTH, east)
    rw = lax.ppermute(s, BOTH, west)
    out, _ = call(
        last_kernel,
        "last",
        (wt, hc, hq, rw, re, q1),
        [(2, LEV, ROWS, 128), state],
        [pltpu.VMEM((2, LEV, ROWS, 128), F32), pltpu.SemaphoreType.DMA((4,))],
        outside=[HBM, VMEM],
        alias={5: 1},
    )
    return out


def solution(mesh):
    plane = P(None, "lat", "lon")
    grid = P(None, None, "lat", "lon")
    return jax.shard_map(
        functools.partial(local, mesh.shape["lat"], mesh.shape["lon"]),
        mesh=mesh,
        in_specs=(grid, plane, plane, plane, plane, plane, P("lon")),
        out_specs=grid,
        check_vma=False,
    )
```

```python
import functools

import jax
import jax.numpy as jnp
from jax import lax
from jax.experimental import pallas as pl
from jax.experimental.pallas import tpu as pltpu
from jax.sharding import PartitionSpec as P

BOTH = ("lat", "lon")
LEV = 3
MEM = 6
ROWS = 256
BLOCKS = 8
GROUPS = 4
TWELFTH = 1.0 / 12.0
F32 = jnp.float32


def lanes():
    return lax.broadcasted_iota(jnp.int32, (8, 128), 1)


def roll(x, shift):
    shift = shift % 128
    return x if shift == 0 else pltpu.roll(x, shift, axis=1)


def face(courant, kappa):
    size = jnp.abs(courant)
    slope = 3.0 * size + kappa
    seven = 7.0 * courant
    return -(courant + size), seven + slope, seven - slope, size - courant


def weigh(ocean, east, west, north, south):
    ea, eb, ec, ed = face(*east)
    wa, wb, wc, wd = face(*west)
    na, nb, nc, nd = face(*north)
    sa, sb, sc, sd = face(*south)
    return (
        ocean + ((wc - eb) + (sc - nb)),
        wa,
        wb - ea,
        wd - ec,
        -ed,
        sa,
        sb - na,
        sd - nc,
        -nd,
    )


def apply(w, q, sides, below2, below1, above1, above2, lane):
    west2 = roll(jnp.where(lane >= 126, sides, q), 2)
    west1 = roll(jnp.where(lane == 127, sides, q), 1)
    east1 = roll(jnp.where(lane == 0, sides, q), -1)
    east2 = roll(jnp.where(lane < 2, sides, q), -2)
    across = (w[1] * west2 + w[2] * west1) + (w[3] * east1 + w[4] * east2)
    along = (w[5] * below2 + w[6] * below1) + (w[7] * above1 + w[8] * above2)
    return w[0] * q + (across + along)


def place(kept, x, source, target, count, lane):
    moved = roll(x, target - source)
    if count == 1:
        here = lane == target
    else:
        here = (lane >= target) & (lane < target + count)
    return jnp.where(here, moved, kept)


def chunk(i, k=0):
    if isinstance(i, int):
        return pl.ds(32 * i + k, 8)
    return pl.ds(pl.multiple_of(32 * i, 32) + k, 8)


def tile(i):
    return pl.ds(8 * i, 8) if isinstance(i, int) else pl.ds(pl.multiple_of(8 * i, 8), 8)


def pack_kernel(
    t_in, ue_in, un_in, ke_in, kn_in, m_in,
    b_ref, e_ref, w_ref, a_ref, f_ref, q0, os, un, kn, ue, ke,
    tv, mv, nb, sb, sems,
):
    half = ROWS // 2
    copies = []
    for n in range(2):
        rows = pl.ds(half * n, half)
        for source, target in (
            (m_in.at[:, rows], mv.at[:, rows]),
            (t_in.at[:, :, rows], tv.at[:, :, rows]),
            (ue_in.at[:, rows], ue.at[:, rows]),
            (ke_in.at[:, rows], ke.at[:, rows]),
        ):
            copies.append(pltpu.make_async_copy(source, target, sems.at[len(copies)]))
    own = pl.ds(8, ROWS)
    copies.append(pltpu.make_async_copy(un_in, un.at[:, own], sems.at[8]))
    copies.append(pltpu.make_async_copy(kn_in, kn.at[:, own], sems.at[9]))
    for c in copies:
        c.start()
    lane = lanes()
    nb[...] = jnp.zeros((64, 128), F32)
    sb[...] = jnp.zeros((64, 128), F32)

    def body(i, carry):
        to_e = jnp.zeros((8, 128), F32)
        to_w = jnp.zeros((8, 128), F32)
        both = jnp.zeros((8, 128), F32)
        for g in range(GROUPS):
            blk, ext = chunk(i, 8 * g), chunk(i, 8 * g + 8)
            for lev in range(LEV):
                ocean = mv[lev, blk].astype(F32)
                os[lev, ext] = ocean
                at = 32 * g + 24 + lev
                to_e = place(to_e, ue[lev, blk] * ocean, 127, at, 1, lane)
                to_e = place(to_e, ke[lev, blk] * ocean, 127, at + 3, 1, lane)
                to_w = place(to_w, ocean, 0, at, 1, lane)
                for t in range(2):
                    m = 3 * t + lev
                    q = tv[t, lev, blk] * ocean
                    q0[m, ext] = q
                    both = place(both, q, 126, 32 * g + 4 * m, 4, lane)
        states = (lane & 31) < 24
        e_ref[tile(i)] = jnp.where(states, both, to_e)
        w_ref[tile(i)] = jnp.where(states, both, to_w)
        return carry

    for n in range(2):
        for c in copies[4 * n : 4 * n + 4]:
            c.wait()
        lax.fori_loop(BLOCKS // 2 * n, BLOCKS // 2 * (n + 1), body, 0)
    for c in copies[8:]:
        c.wait()
    for lev in range(LEV):
        base = 24 + 12 * lev
        for out, lo, rows, faces in ((nb, ROWS - 8, slice(6, 8), slice(5, 7)), (sb, 0, slice(0, 2), slice(0, 2))):
            blk, ext = pl.ds(lo, 8), pl.ds(lo + 8, 8)
            ocean = os[lev, ext]
            beside = jnp.where(lane == 127, 1.0, roll(ocean, -1))
            up = slice(faces.start + 1, faces.stop + 1)
            shut = ocean[faces] * ocean[up]
            u, k = un[lev, ext], kn[lev, ext]
            out[base : base + 2] = u[faces] * shut
            out[base + 3 : base + 5] = k[faces] * shut
            if lo:
                out[base + 2 : base + 3] = u[7:8] * ocean[7:8]
                out[base + 5 : base + 6] = k[7:8] * ocean[7:8]
            open_e = ocean * beside
            out[base + 6 : base + 8] = (ue[lev, blk] * open_e)[rows]
            out[base + 8 : base + 10] = (ke[lev, blk] * open_e)[rows]
            out[base + 10 : base + 12] = ocean[rows]
            for t in range(2):
                m = 3 * t + lev
                q = q0[m, ext]
                out[4 * m : 4 * m + 4] = q[4:8] if lo else q[0:4]
    even = lax.rem(lax.axis_index("lat"), 2) == 0
    north, south = nb[...], sb[...]
    a_ref[...] = jnp.where(even, north, south)
    b_ref[...] = jnp.where(even, south, north)
    f_ref[...] = north


def flip(x):
    return jnp.take_along_axis(x, 127 - lax.broadcasted_iota(jnp.int32, x.shape, 1), axis=1)


def step_kernel(
    ra_ref, rb_ref, re_ref, rw_ref, rf_ref, ue, ke, q0_, os_, un_, kn_,
    q0, os, un, kn, wt, q1, s_ref, hc_ref, hq_ref,
    nh, sh,
):
    lane = lanes()
    lat = lax.axis_index("lat")
    even = lax.rem(lat, 2) == 0
    southern = lat == 0
    northern = lat == lax.axis_size("lat") - 1
    first, second = ra_ref[...], rb_ref[...]
    sh[...] = jnp.where(southern, 0.0, jnp.where(even, second, first))
    nh[...] = jnp.where(even, first, second)

    @pl.when(northern)
    def _():
        f = flip(rf_ref[...])
        shifted = roll(f, -1)
        for m in range(MEM):
            for r in range(4):
                nh[4 * m + r : 4 * m + r + 1] = f[4 * m + 3 - r : 4 * m + 4 - r]
        for lev in range(LEV):
            base = 24 + 12 * lev
            for to, source, x in (
                (0, 1, -f), (1, 0, -f), (2, 2, -f), (3, 4, f), (4, 3, f), (5, 5, f),
                (6, 7, -shifted), (7, 6, -shifted), (8, 9, shifted), (9, 8, shifted), (10, 11, f), (11, 10, f),
            ):
                nh[base + to : base + to + 1] = x[base + source : base + source + 1]

    for m in range(MEM):
        q0[m, 4:8] = sh[4 * m : 4 * m + 4]
        q0[m, 264:268] = nh[4 * m : 4 * m + 4]
    for lev in range(LEV):
        base = 24 + 12 * lev
        top = os[lev, 263:264]
        os[lev, 264:265] = jnp.where(northern, top, nh[base + 10 : base + 11])
        os[lev, 7:8] = sh[base + 11 : base + 12]
        un[lev, 7:8] = sh[base + 2 : base + 3]
        kn[lev, 7:8] = sh[base + 5 : base + 6]

    def weights(i, carry):
        from_w, from_e = re_ref[tile(i)], rw_ref[tile(i)]
        for g in range(GROUPS):
            blk = chunk(i, 8 * g)

            def near(k, g=g):
                return chunk(i, 8 * g + 8 + k)

            for lev in range(LEV):
                ocean = os[lev, near(0)]
                spot = 32 * g + 24 + lev
                beside = jnp.where(lane == 127, roll(from_e, 127 - spot), roll(ocean, -1))
                shut = ocean * beside
                u = ue[lev, blk] * (shut * TWELFTH)
                k = ke[lev, blk] * shut
                uw = jnp.where(lane == 0, roll(from_w, -spot) * (ocean * TWELFTH), roll(u, 1))
                kw = jnp.where(lane == 0, roll(from_w, -(spot + 3)) * ocean, roll(k, 1))
                shut = ocean * os[lev, near(1)]
                north = un[lev, near(0)] * (shut * TWELFTH), kn[lev, near(0)] * shut
                shut = ocean * os[lev, near(-1)]
                south = un[lev, near(-1)] * (shut * TWELFTH), kn[lev, near(-1)] * shut
                w = weigh(ocean, (u, k), (uw, kw), north, south)
                for n in range(9):
                    wt[9 * lev + n, blk] = w[n]
        return carry

    lax.fori_loop(0, BLOCKS, weights, 0)

    def update(i, carry):
        both = jnp.where((lane & 2) == 0, re_ref[tile(i)], rw_ref[tile(i)])
        strip = jnp.zeros((8, 128), F32)
        for g in range(GROUPS):
            blk = chunk(i, 8 * g)

            def near(k, g=g):
                return chunk(i, 8 * g + 8 + k)

            for lev in range(LEV):
                w = [wt[9 * lev + n, blk] for n in range(9)]
                for t in range(2):
                    m = 3 * t + lev
                    spot = 32 * g + 4 * m
                    sides = roll(both, 126 - spot)
                    new = apply(
                        w, q0[m, near(0)], sides, q0[m, near(-2)], q0[m, near(-1)], q0[m, near(1)], q0[m, near(2)], lane
                    )
                    q1[m, near(0)] = new
                    strip = place(strip, new, 126, spot, 4, lane)
        s_ref[tile(i)] = strip
        return carry

    lax.fori_loop(0, BLOCKS, update, 0)
    for m in range(MEM):
        q1[m, 0:8] = jnp.zeros((8, 128), F32)
        q1[m, 264:272] = jnp.zeros((8, 128), F32)

    hc_ref[...] = jnp.zeros((7 * LEV, 8, 128), F32)
    hq_ref[...] = jnp.zeros((5 * MEM, 8, 128), F32)
    for lev in range(LEV):
        base = 24 + 12 * lev
        low = os[lev, 7:8] * os[lev, 8:9]
        high = os[lev, 263:264] * os[lev, 264:265]
        for n, (ref, slot) in enumerate(((un, 0), (kn, 3))):
            lower = jnp.where(northern, nh[base + slot + 2 : base + slot + 3], ref[lev, 263:264] * high)
            hc_ref[7 * lev + n, 0:2] = sh[base + slot : base + slot + 2]
            hc_ref[7 * lev + n, 2:3] = lower
            hc_ref[7 * lev + n, 3:4] = nh[base + slot : base + slot + 1]
            hc_ref[7 * lev + 2 + n, 0:1] = sh[base + slot + 1 : base + slot + 2]
            hc_ref[7 * lev + 2 + n, 1:2] = ref[lev, 7:8] * low
            hc_ref[7 * lev + 2 + n, 2:4] = nh[base + slot : base + slot + 2]
        for n in range(3):
            hc_ref[7 * lev + 4 + n, 0:2] = sh[base + 6 + 2 * n : base + 8 + 2 * n]
            hc_ref[7 * lev + 4 + n, 2:4] = nh[base + 6 + 2 * n : base + 8 + 2 * n]
    for m in range(MEM):
        for k in range(5):
            hq_ref[6 * k + m, 0:2] = q0[m, 4 + k : 6 + k]
            hq_ref[6 * k + m, 2:4] = q0[m, 262 + k : 264 + k]
    strip = jnp.zeros((8, 128), F32)
    for m in range(MEM):
        strip = place(strip, hq_ref[12 + m], 126, 4 * m, 4, lane)
    for lev in range(LEV):
        u, k, ocean = hc_ref[7 * lev + 4], hc_ref[7 * lev + 5], hc_ref[7 * lev + 6]
        strip = place(strip, u, 127, 32 + lev, 1, lane)
        strip = place(strip, k, 127, 35 + lev, 1, lane)
        strip = place(strip, ocean, 127, 38 + 2 * lev, 2, lane)
    s_ref[64:72] = strip


def inside_kernel(wt, q1, part, p_ref, r_ref):
    lane = lanes()
    low = lane < 64

    def body(i, carry):
        far = jnp.zeros((8, 128), F32)
        close = jnp.zeros((8, 128), F32)
        nothing = jnp.zeros((8, 128), F32)
        for g in range(GROUPS):
            blk = chunk(i, 8 * g)

            def near(k, g=g):
                return chunk(i, 8 * g + 8 + k)

            for lev in range(LEV):
                w = [wt[9 * lev + n, blk] for n in range(9)]
                outer = jnp.where(low, w[1], w[4])
                inner = jnp.where(low, w[2], w[3])
                for t in range(2):
                    m = 3 * t + lev
                    spot = 32 * g + 4 * m
                    far = place(far, outer, 126, spot, 4, lane)
                    close = place(close, inner, 126, spot, 4, lane)
                    part[t, lev, blk] = apply(
                        w, q1[m, near(0)], nothing, q1[m, near(-2)], q1[m, near(-1)], q1[m, near(1)], q1[m, near(2)], lane
                    )
        p_ref[tile(i)] = far
        r_ref[tile(i)] = close
        return carry

    lax.fori_loop(0, BLOCKS, body, 0)


def last_kernel(wt, hc_ref, hq_ref, rw_ref, re_ref, p_ref, r_ref, q1_, part_, out_ref, q1, new_ref, added, sems):
    lane = lanes()
    row = lax.broadcasted_iota(jnp.int32, (8, 128), 0)
    northern = lax.axis_index("lat") == lax.axis_size("lat") - 1
    folded = (row >= 2) & northern
    wide = lax.broadcasted_iota(jnp.int32, (8 * BLOCKS, 128), 1)
    slot = wide & 3
    own = pl.ds(0, 8 * BLOCKS)
    beyond = jnp.where(slot < 2, roll(rw_ref[own], -2), roll(re_ref[own], 2))
    beside = jnp.where(slot == 1, roll(beyond, 1), jnp.where(slot == 2, roll(beyond, -1), 0.0))
    added[...] = p_ref[...] * beyond + r_ref[...] * beside
    ends = (lane < 2) | (lane >= 126)

    def body(i, carry):
        terms = added[tile(i)]
        for g in range(GROUPS):
            blk = chunk(i, 8 * g)
            for lev in range(LEV):
                for t in range(2):
                    more = roll(terms, 126 - 32 * g - 4 * (3 * t + lev))
                    new_ref[t, lev, blk] = new_ref[t, lev, blk] + jnp.where(ends, more, 0.0)
        return carry

    parts = []

    def leave(first, count):
        rows = pl.ds(first, count)
        part = pltpu.make_async_copy(new_ref.at[:, :, rows], out_ref.at[:, :, rows], sems.at[len(parts)])
        part.start()
        parts.append(part)

    lax.fori_loop(2, 6, body, 0)
    leave(64, 128)
    lax.fori_loop(0, 2, body, 0)
    lax.fori_loop(6, 8, body, 0)
    from_w, from_e = re_ref[64:72], rw_ref[64:72]
    both = jnp.where((lane & 2) == 0, from_w, from_e)
    for lev in range(LEV):
        ulo, klo, uup, kup, u, k, ocean = (hc_ref[7 * lev + n] for n in range(7))
        ocean_w = roll(from_w, -(38 + 2 * lev))
        ocean_e = roll(from_e, 127 - 39 - 2 * lev)

        def ends(x, spot, ocean=ocean, ocean_w=ocean_w, ocean_e=ocean_e):
            east = jnp.where(folded, roll(from_e, 127 - spot) * ocean, x * ocean_e)
            west = jnp.where(folded, roll(x, 1) * ocean_w, roll(from_w, -spot) * ocean)
            return jnp.where(lane == 127, east, x), jnp.where(lane == 0, west, roll(x, 1))

        ue, uw = ends(u, 32 + lev)
        ke, kw = ends(k, 35 + lev)
        w = weigh(ocean, (ue * TWELFTH, ke), (uw * TWELFTH, kw), (uup * TWELFTH, kup), (ulo * TWELFTH, klo))
        for t in range(2):
            m = 3 * t + lev
            q = [hq_ref[6 * n + m] for n in range(5)]
            new = apply(w, q[2], roll(both, 126 - 4 * m), q[0], q[1], q[3], q[4], lane)
            q1[m, 6:8] = new[0:2]
            q1[m, 264:266] = new[2:4]

    for i, g in ((0, 0), (BLOCKS - 1, GROUPS - 1)):
        both = jnp.where((lane & 2) == 0, re_ref[tile(i)], rw_ref[tile(i)])
        blk = chunk(i, 8 * g)
        for lev in range(LEV):
            w = [wt[9 * lev + n, blk] for n in range(9)]
            for t in range(2):
                m = 3 * t + lev
                sides = roll(both, 126 - 32 * g - 4 * m)
                q = [q1[m, chunk(i, 8 * g + 8 + k)] for k in (-2, -1, 0, 1, 2)]
                new_ref[t, lev, blk] = apply(w, q[2], sides, q[0], q[1], q[3], q[4], lane)
    leave(0, 64)
    leave(192, 64)
    for part in parts:
        part.wait()


VMEM = pl.BlockSpec(memory_space=pltpu.VMEM)
HBM = pl.BlockSpec(memory_space=pltpu.HBM)


def call(kernel, name, operands, shapes, scratch=(), inside=VMEM, outside=None, alias=None, cost=None):
    return pl.pallas_call(
        kernel,
        out_shape=[jax.ShapeDtypeStruct(s, F32) for s in shapes],
        in_specs=[inside] * len(operands),
        out_specs=outside or [VMEM] * len(shapes),
        scratch_shapes=list(scratch),
        input_output_aliases=alias or {},
        cost_estimate=cost,
        compiler_params=pltpu.CompilerParams(vmem_limit_bytes=16 * 2**20),
        name=name,
    )(*operands)


def patterns(height, width):
    def flat(make):
        return [
            (lat * width + lon, (to[0] % height) * width + to[1] % width)
            for lat in range(height)
            for lon in range(width)
            for to in [make(lat, lon)]
        ]

    def odd(lat, lon):
        if lat in (0, height - 1):
            return lat, lon
        return (lat + 1, lon) if lat % 2 else (lat - 1, lon)

    def fold(pivot):
        top = (height - 1) * width
        still = [(n, n) for n in range(top)]
        return still + [(top + lon, top + (pivot - 1 - lon) % width) for lon in range(width)]

    east = flat(lambda lat, lon: (lat, lon + 1))
    west = flat(lambda lat, lon: (lat, lon - 1))
    pairs = flat(lambda lat, lon: (lat + 1, lon) if lat % 2 == 0 else (lat - 1, lon))
    return east, west, pairs, flat(odd), fold


def local(height, width, tracers, east_courant, north_courant, east_kappa, north_kappa, ocean_mask, fold_map):
    east, west, pairs, odd, fold = patterns(height, width)
    fields = (tracers, east_courant, north_courant, east_kappa, north_kappa, ocean_mask)
    pivot = ((fold_map[0] + 1) // 128 + lax.axis_index("lon")) % width
    edge, side = (64, 128), (72, 128)
    ext, own, state = (LEV, ROWS + 16, 128), (LEV, ROWS, 128), (MEM, ROWS + 16, 128)
    b, e, w, a, f, q0, os, un, kn, ue, ke = call(
        pack_kernel,
        "pack",
        [pltpu.with_memory_space_constraint(x, pltpu.HBM) for x in fields],
        [edge] * 5 + [state, ext, ext, ext, own, own],
        [
            pltpu.VMEM((2, LEV, ROWS, 128), F32),
            pltpu.VMEM((LEV, ROWS, 128), jnp.int32),
            pltpu.VMEM(edge, F32),
            pltpu.VMEM(edge, F32),
            pltpu.SemaphoreType.DMA((10,)),
        ],
        inside=HBM,
    )
    weights = (9 * LEV, ROWS, 128)

    rb = lax.ppermute(b, BOTH, odd)
    re = lax.ppermute(e, BOTH, east)
    rw = lax.ppermute(w, BOTH, west)
    ra = lax.ppermute(a, BOTH, pairs)
    rf = lax.switch(pivot, [lambda x, p=p: lax.ppermute(x, BOTH, fold(p)) for p in range(width)], f)
    q0, os, un, kn, wt, q1, s, hc, hq = call(
        step_kernel,
        "step",
        (ra, rb, re, rw, rf, ue, ke, q0, os, un, kn),
        [state, ext, ext, ext, weights, state, side, (7 * LEV, 8, 128), (5 * MEM, 8, 128)],
        [pltpu.VMEM(edge, F32), pltpu.VMEM(edge, F32)],
        alias={7 + n: n for n in range(4)},
    )
    re = lax.ppermute(s, BOTH, east)
    rw = lax.ppermute(s, BOTH, west)
    strips = (8 * BLOCKS, 128)
    part, far, close = call(
        inside_kernel,
        "inside",
        (wt, q1),
        [(2, LEV, ROWS, 128), strips, strips],
        cost=pl.CostEstimate(flops=20 * MEM * ROWS * 128, bytes_accessed=6 * 2**20, transcendentals=0),
    )
    out, _, _ = call(
        last_kernel,
        "last",
        (wt, hc, hq, rw, re, far, close, q1, part),
        [(2, LEV, ROWS, 128), state, (2, LEV, ROWS, 128)],
        [pltpu.VMEM(strips, F32), pltpu.SemaphoreType.DMA((3,))],
        outside=[HBM, VMEM, VMEM],
        alias={7: 1, 8: 2},
    )
    return out


def solution(mesh):
    plane = P(None, "lat", "lon")
    grid = P(None, None, "lat", "lon")
    return jax.shard_map(
        functools.partial(local, mesh.shape["lat"], mesh.shape["lon"]),
        mesh=mesh,
        in_specs=(grid, plane, plane, plane, plane, plane, P("lon")),
        out_specs=grid,
        check_vma=False,
    )
```

```python
import functools

import jax
import jax.numpy as jnp
from jax import lax
from jax.experimental import pallas as pl
from jax.experimental.pallas import tpu as pltpu
from jax.sharding import PartitionSpec as P

BOTH = ("lat", "lon")
LEV = 3
MEM = 6
ROWS = 256
BLOCKS = 8
GROUPS = 4
TWELFTH = 1.0 / 12.0
F32 = jnp.float32


def lanes():
    return lax.broadcasted_iota(jnp.int32, (8, 128), 1)


def roll(x, shift):
    shift = shift % 128
    return x if shift == 0 else pltpu.roll(x, shift, axis=1)


def face(courant, kappa):
    size = jnp.abs(courant)
    slope = 3.0 * size + kappa
    seven = 7.0 * courant
    return -(courant + size), seven + slope, seven - slope, size - courant


def weigh(ocean, east, west, north, south):
    ea, eb, ec, ed = face(*east)
    wa, wb, wc, wd = face(*west)
    na, nb, nc, nd = face(*north)
    sa, sb, sc, sd = face(*south)
    return (
        ocean + ((wc - eb) + (sc - nb)),
        wa,
        wb - ea,
        wd - ec,
        -ed,
        sa,
        sb - na,
        sd - nc,
        -nd,
    )


def apply(w, q, sides, below2, below1, above1, above2, lane):
    west2 = roll(jnp.where(lane >= 126, sides, q), 2)
    west1 = roll(jnp.where(lane == 127, sides, q), 1)
    east1 = roll(jnp.where(lane == 0, sides, q), -1)
    east2 = roll(jnp.where(lane < 2, sides, q), -2)
    across = (w[1] * west2 + w[2] * west1) + (w[3] * east1 + w[4] * east2)
    along = (w[5] * below2 + w[6] * below1) + (w[7] * above1 + w[8] * above2)
    return w[0] * q + (across + along)


def place(kept, x, source, target, count, lane):
    moved = roll(x, target - source)
    if count == 1:
        here = lane == target
    else:
        here = (lane >= target) & (lane < target + count)
    return jnp.where(here, moved, kept)


def chunk(i, k=0):
    if isinstance(i, int):
        return pl.ds(32 * i + k, 8)
    return pl.ds(pl.multiple_of(32 * i, 32) + k, 8)


def tile(i):
    return pl.ds(8 * i, 8) if isinstance(i, int) else pl.ds(pl.multiple_of(8 * i, 8), 8)


def pack_kernel(
    t_in, ue_in, un_in, ke_in, kn_in, m_in,
    b_ref, e_ref, w_ref, a_ref, f_ref, q0, os, un, kn, ue, ke,
    tv, mv, nb, sb, sems,
):
    half = ROWS // 2
    copies = []
    for n in range(2):
        rows = pl.ds(half * n, half)
        for source, target in (
            (m_in.at[:, rows], mv.at[:, rows]),
            (t_in.at[:, :, rows], tv.at[:, :, rows]),
            (ue_in.at[:, rows], ue.at[:, rows]),
            (ke_in.at[:, rows], ke.at[:, rows]),
        ):
            copies.append(pltpu.make_async_copy(source, target, sems.at[len(copies)]))
    own = pl.ds(8, ROWS)
    copies.append(pltpu.make_async_copy(un_in, un.at[:, own], sems.at[8]))
    copies.append(pltpu.make_async_copy(kn_in, kn.at[:, own], sems.at[9]))
    for c in copies:
        c.start()
    lane = lanes()
    nb[...] = jnp.zeros((64, 128), F32)
    sb[...] = jnp.zeros((64, 128), F32)

    def body(i, carry):
        to_e = jnp.zeros((8, 128), F32)
        to_w = jnp.zeros((8, 128), F32)
        both = jnp.zeros((8, 128), F32)
        for g in range(GROUPS):
            blk, ext = chunk(i, 8 * g), chunk(i, 8 * g + 8)
            for lev in range(LEV):
                ocean = mv[lev, blk].astype(F32)
                os[lev, ext] = ocean
                at = 32 * g + 24 + lev
                to_e = place(to_e, ue[lev, blk] * ocean, 127, at, 1, lane)
                to_e = place(to_e, ke[lev, blk] * ocean, 127, at + 3, 1, lane)
                to_w = place(to_w, ocean, 0, at, 1, lane)
                for t in range(2):
                    m = 3 * t + lev
                    q = tv[t, lev, blk] * ocean
                    q0[m, ext] = q
                    both = place(both, q, 126, 32 * g + 4 * m, 4, lane)
        states = (lane & 31) < 24
        e_ref[tile(i)] = jnp.where(states, both, to_e)
        w_ref[tile(i)] = jnp.where(states, both, to_w)
        return carry

    for n in range(2):
        for c in copies[4 * n : 4 * n + 4]:
            c.wait()
        lax.fori_loop(BLOCKS // 2 * n, BLOCKS // 2 * (n + 1), body, 0)
    for c in copies[8:]:
        c.wait()
    for lev in range(LEV):
        base = 24 + 12 * lev
        for out, lo, rows, faces in ((nb, ROWS - 8, slice(6, 8), slice(5, 7)), (sb, 0, slice(0, 2), slice(0, 2))):
            blk, ext = pl.ds(lo, 8), pl.ds(lo + 8, 8)
            ocean = os[lev, ext]
            beside = jnp.where(lane == 127, 1.0, roll(ocean, -1))
            up = slice(faces.start + 1, faces.stop + 1)
            shut = ocean[faces] * ocean[up]
            u, k = un[lev, ext], kn[lev, ext]
            out[base : base + 2] = u[faces] * shut
            out[base + 3 : base + 5] = k[faces] * shut
            if lo:
                out[base + 2 : base + 3] = u[7:8] * ocean[7:8]
                out[base + 5 : base + 6] = k[7:8] * ocean[7:8]
            open_e = ocean * beside
            out[base + 6 : base + 8] = (ue[lev, blk] * open_e)[rows]
            out[base + 8 : base + 10] = (ke[lev, blk] * open_e)[rows]
            out[base + 10 : base + 12] = ocean[rows]
            for t in range(2):
                m = 3 * t + lev
                q = q0[m, ext]
                out[4 * m : 4 * m + 4] = q[4:8] if lo else q[0:4]
    even = lax.rem(lax.axis_index("lat"), 2) == 0
    north, south = nb[...], sb[...]
    a_ref[...] = jnp.where(even, north, south)
    b_ref[...] = jnp.where(even, south, north)
    f_ref[...] = north


def flip(x):
    return jnp.take_along_axis(x, 127 - lax.broadcasted_iota(jnp.int32, x.shape, 1), axis=1)


def step_kernel(
    ra_ref, rb_ref, re_ref, rw_ref, rf_ref, ue, ke, q0_, os_, un_, kn_,
    q0, os, un, kn, wt, q1, s_ref, hc_ref, hq_ref,
    nh, sh, fv, sem,
):
    lane = lanes()
    lat = lax.axis_index("lat")
    even = lax.rem(lat, 2) == 0
    southern = lat == 0
    northern = lat == lax.axis_size("lat") - 1
    arrival = pltpu.make_async_copy(rf_ref, fv, sem)
    arrival.start()
    first, second = ra_ref[...], rb_ref[...]
    sh[...] = jnp.where(southern, 0.0, jnp.where(even, second, first))
    nh[...] = jnp.where(even, first, second)

    for lev in range(LEV):
        base = 24 + 12 * lev
        top = os[lev, 263:264]
        os[lev, 264:265] = jnp.where(northern, top, nh[base + 10 : base + 11])
        os[lev, 7:8] = sh[base + 11 : base + 12]
        un[lev, 7:8] = sh[base + 2 : base + 3]
        kn[lev, 7:8] = sh[base + 5 : base + 6]

    def weights(i, carry):
        from_w, from_e = re_ref[tile(i)], rw_ref[tile(i)]
        for g in range(GROUPS):
            blk = chunk(i, 8 * g)

            def near(k, g=g):
                return chunk(i, 8 * g + 8 + k)

            for lev in range(LEV):
                ocean = os[lev, near(0)]
                spot = 32 * g + 24 + lev
                beside = jnp.where(lane == 127, roll(from_e, 127 - spot), roll(ocean, -1))
                shut = ocean * beside
                u = ue[lev, blk] * (shut * TWELFTH)
                k = ke[lev, blk] * shut
                uw = jnp.where(lane == 0, roll(from_w, -spot) * (ocean * TWELFTH), roll(u, 1))
                kw = jnp.where(lane == 0, roll(from_w, -(spot + 3)) * ocean, roll(k, 1))
                shut = ocean * os[lev, near(1)]
                north = un[lev, near(0)] * (shut * TWELFTH), kn[lev, near(0)] * shut
                shut = ocean * os[lev, near(-1)]
                south = un[lev, near(-1)] * (shut * TWELFTH), kn[lev, near(-1)] * shut
                w = weigh(ocean, (u, k), (uw, kw), north, south)
                for n in range(9):
                    wt[9 * lev + n, blk] = w[n]
        return carry

    lax.fori_loop(0, BLOCKS, weights, 0)
    arrival.wait()

    @pl.when(northern)
    def _():
        f = flip(fv[...])
        shifted = roll(f, -1)
        for m in range(MEM):
            for r in range(4):
                nh[4 * m + r : 4 * m + r + 1] = f[4 * m + 3 - r : 4 * m + 4 - r]
        for lev in range(LEV):
            base = 24 + 12 * lev
            for to, source, x in (
                (0, 1, -f), (1, 0, -f), (2, 2, -f), (3, 4, f), (4, 3, f), (5, 5, f),
                (6, 7, -shifted), (7, 6, -shifted), (8, 9, shifted), (9, 8, shifted), (10, 11, f), (11, 10, f),
            ):
                nh[base + to : base + to + 1] = x[base + source : base + source + 1]

    for m in range(MEM):
        q0[m, 4:8] = sh[4 * m : 4 * m + 4]
        q0[m, 264:268] = nh[4 * m : 4 * m + 4]

    def update(i, carry):
        both = jnp.where((lane & 2) == 0, re_ref[tile(i)], rw_ref[tile(i)])
        strip = jnp.zeros((8, 128), F32)
        for g in range(GROUPS):
            blk = chunk(i, 8 * g)

            def near(k, g=g):
                return chunk(i, 8 * g + 8 + k)

            for lev in range(LEV):
                w = [wt[9 * lev + n, blk] for n in range(9)]
                for t in range(2):
                    m = 3 * t + lev
                    spot = 32 * g + 4 * m
                    sides = roll(both, 126 - spot)
                    new = apply(
                        w, q0[m, near(0)], sides, q0[m, near(-2)], q0[m, near(-1)], q0[m, near(1)], q0[m, near(2)], lane
                    )
                    q1[m, near(0)] = new
                    strip = place(strip, new, 126, spot, 4, lane)
        s_ref[tile(i)] = strip
        return carry

    lax.fori_loop(0, BLOCKS, update, 0)
    for m in range(MEM):
        q1[m, 0:8] = jnp.zeros((8, 128), F32)
        q1[m, 264:272] = jnp.zeros((8, 128), F32)

    hc_ref[...] = jnp.zeros((7 * LEV, 8, 128), F32)
    hq_ref[...] = jnp.zeros((5 * MEM, 8, 128), F32)
    for lev in range(LEV):
        base = 24 + 12 * lev
        low = os[lev, 7:8] * os[lev, 8:9]
        high = os[lev, 263:264] * os[lev, 264:265]
        for n, (ref, slot) in enumerate(((un, 0), (kn, 3))):
            lower = jnp.where(northern, nh[base + slot + 2 : base + slot + 3], ref[lev, 263:264] * high)
            hc_ref[7 * lev + n, 0:2] = sh[base + slot : base + slot + 2]
            hc_ref[7 * lev + n, 2:3] = lower
            hc_ref[7 * lev + n, 3:4] = nh[base + slot : base + slot + 1]
            hc_ref[7 * lev + 2 + n, 0:1] = sh[base + slot + 1 : base + slot + 2]
            hc_ref[7 * lev + 2 + n, 1:2] = ref[lev, 7:8] * low
            hc_ref[7 * lev + 2 + n, 2:4] = nh[base + slot : base + slot + 2]
        for n in range(3):
            hc_ref[7 * lev + 4 + n, 0:2] = sh[base + 6 + 2 * n : base + 8 + 2 * n]
            hc_ref[7 * lev + 4 + n, 2:4] = nh[base + 6 + 2 * n : base + 8 + 2 * n]
    for m in range(MEM):
        for k in range(5):
            hq_ref[6 * k + m, 0:2] = q0[m, 4 + k : 6 + k]
            hq_ref[6 * k + m, 2:4] = q0[m, 262 + k : 264 + k]
    strip = jnp.zeros((8, 128), F32)
    for m in range(MEM):
        strip = place(strip, hq_ref[12 + m], 126, 4 * m, 4, lane)
    for lev in range(LEV):
        u, k, ocean = hc_ref[7 * lev + 4], hc_ref[7 * lev + 5], hc_ref[7 * lev + 6]
        strip = place(strip, u, 127, 32 + lev, 1, lane)
        strip = place(strip, k, 127, 35 + lev, 1, lane)
        strip = place(strip, ocean, 127, 38 + 2 * lev, 2, lane)
    s_ref[64:72] = strip


def inside_kernel(wt, q1, part, p_ref, r_ref):
    lane = lanes()
    low = lane < 64

    def body(i, carry):
        far = jnp.zeros((8, 128), F32)
        close = jnp.zeros((8, 128), F32)
        nothing = jnp.zeros((8, 128), F32)
        for g in range(GROUPS):
            blk = chunk(i, 8 * g)

            def near(k, g=g):
                return chunk(i, 8 * g + 8 + k)

            for lev in range(LEV):
                w = [wt[9 * lev + n, blk] for n in range(9)]
                outer = jnp.where(low, w[1], w[4])
                inner = jnp.where(low, w[2], w[3])
                for t in range(2):
                    m = 3 * t + lev
                    spot = 32 * g + 4 * m
                    far = place(far, outer, 126, spot, 4, lane)
                    close = place(close, inner, 126, spot, 4, lane)
                    part[t, lev, blk] = apply(
                        w, q1[m, near(0)], nothing, q1[m, near(-2)], q1[m, near(-1)], q1[m, near(1)], q1[m, near(2)], lane
                    )
        p_ref[tile(i)] = far
        r_ref[tile(i)] = close
        return carry

    lax.fori_loop(0, BLOCKS, body, 0)


def last_kernel(wt, hc_ref, hq_ref, rw_ref, re_ref, p_ref, r_ref, q1_, part_, out_ref, q1, new_ref, added, sems):
    lane = lanes()
    row = lax.broadcasted_iota(jnp.int32, (8, 128), 0)
    northern = lax.axis_index("lat") == lax.axis_size("lat") - 1
    folded = (row >= 2) & northern
    wide = lax.broadcasted_iota(jnp.int32, (8 * BLOCKS, 128), 1)
    slot = wide & 3
    own = pl.ds(0, 8 * BLOCKS)
    beyond = jnp.where(slot < 2, roll(rw_ref[own], -2), roll(re_ref[own], 2))
    beside = jnp.where(slot == 1, roll(beyond, 1), jnp.where(slot == 2, roll(beyond, -1), 0.0))
    added[...] = p_ref[...] * beyond + r_ref[...] * beside
    ends = (lane < 2) | (lane >= 126)

    def body(i, carry):
        terms = added[tile(i)]
        for g in range(GROUPS):
            blk = chunk(i, 8 * g)
            for lev in range(LEV):
                for t in range(2):
                    more = roll(terms, 126 - 32 * g - 4 * (3 * t + lev))
                    new_ref[t, lev, blk] = new_ref[t, lev, blk] + jnp.where(ends, more, 0.0)
        return carry

    parts = []

    def leave(first, count):
        rows = pl.ds(first, count)
        part = pltpu.make_async_copy(new_ref.at[:, :, rows], out_ref.at[:, :, rows], sems.at[len(parts)])
        part.start()
        parts.append(part)

    lax.fori_loop(2, 6, body, 0)
    leave(64, 128)
    lax.fori_loop(0, 2, body, 0)
    lax.fori_loop(6, 8, body, 0)
    from_w, from_e = re_ref[64:72], rw_ref[64:72]
    both = jnp.where((lane & 2) == 0, from_w, from_e)
    for lev in range(LEV):
        ulo, klo, uup, kup, u, k, ocean = (hc_ref[7 * lev + n] for n in range(7))
        ocean_w = roll(from_w, -(38 + 2 * lev))
        ocean_e = roll(from_e, 127 - 39 - 2 * lev)

        def ends(x, spot, ocean=ocean, ocean_w=ocean_w, ocean_e=ocean_e):
            east = jnp.where(folded, roll(from_e, 127 - spot) * ocean, x * ocean_e)
            west = jnp.where(folded, roll(x, 1) * ocean_w, roll(from_w, -spot) * ocean)
            return jnp.where(lane == 127, east, x), jnp.where(lane == 0, west, roll(x, 1))

        ue, uw = ends(u, 32 + lev)
        ke, kw = ends(k, 35 + lev)
        w = weigh(ocean, (ue * TWELFTH, ke), (uw * TWELFTH, kw), (uup * TWELFTH, kup), (ulo * TWELFTH, klo))
        for t in range(2):
            m = 3 * t + lev
            q = [hq_ref[6 * n + m] for n in range(5)]
            new = apply(w, q[2], roll(both, 126 - 4 * m), q[0], q[1], q[3], q[4], lane)
            q1[m, 6:8] = new[0:2]
            q1[m, 264:266] = new[2:4]

    for i, g in ((0, 0), (BLOCKS - 1, GROUPS - 1)):
        both = jnp.where((lane & 2) == 0, re_ref[tile(i)], rw_ref[tile(i)])
        blk = chunk(i, 8 * g)
        for lev in range(LEV):
            w = [wt[9 * lev + n, blk] for n in range(9)]
            for t in range(2):
                m = 3 * t + lev
                sides = roll(both, 126 - 32 * g - 4 * m)
                q = [q1[m, chunk(i, 8 * g + 8 + k)] for k in (-2, -1, 0, 1, 2)]
                new_ref[t, lev, blk] = apply(w, q[2], sides, q[0], q[1], q[3], q[4], lane)
    leave(0, 64)
    leave(192, 64)
    for part in parts:
        part.wait()


VMEM = pl.BlockSpec(memory_space=pltpu.VMEM)
HBM = pl.BlockSpec(memory_space=pltpu.HBM)


def call(kernel, name, operands, shapes, scratch=(), inside=VMEM, outside=None, alias=None, cost=None):
    return pl.pallas_call(
        kernel,
        out_shape=[jax.ShapeDtypeStruct(s, F32) for s in shapes],
        in_specs=inside if isinstance(inside, list) else [inside] * len(operands),
        out_specs=outside or [VMEM] * len(shapes),
        scratch_shapes=list(scratch),
        input_output_aliases=alias or {},
        cost_estimate=cost,
        compiler_params=pltpu.CompilerParams(vmem_limit_bytes=16 * 2**20),
        name=name,
    )(*operands)


def patterns(height, width):
    def flat(make):
        return [
            (lat * width + lon, (to[0] % height) * width + to[1] % width)
            for lat in range(height)
            for lon in range(width)
            for to in [make(lat, lon)]
        ]

    def odd(lat, lon):
        if lat in (0, height - 1):
            return lat, lon
        return (lat + 1, lon) if lat % 2 else (lat - 1, lon)

    def fold(pivot):
        top = (height - 1) * width
        still = [(n, n) for n in range(top)]
        return still + [(top + lon, top + (pivot - 1 - lon) % width) for lon in range(width)]

    east = flat(lambda lat, lon: (lat, lon + 1))
    west = flat(lambda lat, lon: (lat, lon - 1))
    pairs = flat(lambda lat, lon: (lat + 1, lon) if lat % 2 == 0 else (lat - 1, lon))
    return east, west, pairs, flat(odd), fold


def local(height, width, tracers, east_courant, north_courant, east_kappa, north_kappa, ocean_mask, fold_map):
    east, west, pairs, odd, fold = patterns(height, width)
    fields = (tracers, east_courant, north_courant, east_kappa, north_kappa, ocean_mask)
    pivot = ((fold_map[0] + 1) // 128 + lax.axis_index("lon")) % width
    edge, side = (64, 128), (72, 128)
    ext, own, state = (LEV, ROWS + 16, 128), (LEV, ROWS, 128), (MEM, ROWS + 16, 128)
    b, e, w, a, f, q0, os, un, kn, ue, ke = call(
        pack_kernel,
        "pack",
        [pltpu.with_memory_space_constraint(x, pltpu.HBM) for x in fields],
        [edge] * 5 + [state, ext, ext, ext, own, own],
        [
            pltpu.VMEM((2, LEV, ROWS, 128), F32),
            pltpu.VMEM((LEV, ROWS, 128), jnp.int32),
            pltpu.VMEM(edge, F32),
            pltpu.VMEM(edge, F32),
            pltpu.SemaphoreType.DMA((10,)),
        ],
        inside=HBM,
    )
    weights = (9 * LEV, ROWS, 128)

    rb = lax.ppermute(b, BOTH, odd)
    re = lax.ppermute(e, BOTH, east)
    rw = lax.ppermute(w, BOTH, west)
    ra = lax.ppermute(a, BOTH, pairs)
    rf = lax.switch(pivot, [lambda x, p=p: lax.ppermute(x, BOTH, fold(p)) for p in range(width)], f)
    q0, os, un, kn, wt, q1, s, hc, hq = call(
        step_kernel,
        "step",
        (ra, rb, re, rw, pltpu.with_memory_space_constraint(rf, pltpu.HBM), ue, ke, q0, os, un, kn),
        [state, ext, ext, ext, weights, state, side, (7 * LEV, 8, 128), (5 * MEM, 8, 128)],
        [pltpu.VMEM(edge, F32), pltpu.VMEM(edge, F32), pltpu.VMEM(edge, F32), pltpu.SemaphoreType.DMA],
        inside=[VMEM] * 4 + [HBM] + [VMEM] * 6,
        alias={7 + n: n for n in range(4)},
    )
    re = lax.ppermute(s, BOTH, east)
    rw = lax.ppermute(s, BOTH, west)
    strips = (8 * BLOCKS, 128)
    part, far, close = call(
        inside_kernel,
        "inside",
        (wt, q1),
        [(2, LEV, ROWS, 128), strips, strips],
        cost=pl.CostEstimate(flops=20 * MEM * ROWS * 128, bytes_accessed=6 * 2**20, transcendentals=0),
    )
    out, _, _ = call(
        last_kernel,
        "last",
        (wt, hc, hq, rw, re, far, close, q1, part),
        [(2, LEV, ROWS, 128), state, (2, LEV, ROWS, 128)],
        [pltpu.VMEM(strips, F32), pltpu.SemaphoreType.DMA((3,))],
        outside=[HBM, VMEM, VMEM],
        alias={7: 1, 8: 2},
    )
    return out


def solution(mesh):
    plane = P(None, "lat", "lon")
    grid = P(None, None, "lat", "lon")
    return jax.shard_map(
        functools.partial(local, mesh.shape["lat"], mesh.shape["lon"]),
        mesh=mesh,
        in_specs=(grid, plane, plane, plane, plane, plane, P("lon")),
        out_specs=grid,
        check_vma=False,
    )
```
